32 devices in a mesh: expert: 8 (over z, y), slot: 4 (over x, core).
Axes of the slice: x: 2, y: 2, z: 4, core: 2. Of those that a mesh axis runs over, the one named last changes fastest.
Arguments:
- tokens: bfloat16 [4096, 2048], P(('expert', 'slot')), may hold values from -6 to 6
- out_grad: bfloat16 [4096, 2048], P(('expert', 'slot')), may hold values from -6 to 6
- routing: int32 [4096, 1], P(('expert', 'slot')), may hold values from 0 to 7; in each aligned block of 128 rows (0 to 127, 128 to 255, ...) at most 32 rows name the same one
- plan: int32 [8], replicated, may hold values from 0 to 5, as said below
- gate_weight: bfloat16 [8, 2048, 768], P('expert', None, 'slot'), as said below
- up_weight: bfloat16 [8, 2048, 768], P('expert', None, 'slot'), as said below
- down_weight: bfloat16 [8, 768, 2048], P('expert', 'slot'), as said below
- master: float32 [6, 768, 2048], P(None, ('slot', 'expert'))
- moment: float32 [6, 768, 2048], P(None, ('slot', 'expert')), may hold values from -24 to 24
- second: float32 [6, 768, 2048], P(None, ('slot', 'expert')), may hold values from 1 to 400
Outputs:
- token_grad: bfloat16 [4096, 2048], P(('expert', 'slot'))
- new_master: float32 [6, 768, 2048], P(None, ('slot', 'expert'))
- new_moment: float32 [6, 768, 2048], P(None, ('slot', 'expert'))
- new_second: float32 [6, 768, 2048], P(None, ('slot', 'expert'))
- new_down: bfloat16 [8, 768, 2048], P('expert', 'slot')
The draws below stay inside these ranges and needn't reach their ends.
Inputs may be any that keep to these rules, and one draw needn't show every extreme that they name: `routing`: in the rows of one device no slot is named more than 32 times, a bound that some block reaches. `plan`: every expert 0 to 5 is held by at least one slot. `gate_weight`: slots holding the same expert have equal gate and up projections. `up_weight`: slots holding the same expert have equal gate and up projections. down_weight[k] is master[plan[k]] rounded to bfloat16.
All inputs are finite; a program needn't handle non-finite values.
Results may differ from the reference program's by a relative error of at most 0.012.
Values may be sent and summed in bfloat16 or wider, within the bound.
No kernel may reach another device: no remote copies, remote signals or barrier semaphores. Data moves between devices by JAX's collectives and lax.ppermute only.
A program may use at most 128 MiB of HBM per device.

```python
import math
import jax
import jax.numpy as jnp
import numpy as np
from jax import lax

D = 2048
FF = 768
TOK_DEV = 128
SLOTS = 8
PRIM = 6
CAP = 32
TOKENS = 4096
N_EXPERT = 8
N_SLOT = 4


def plan_from(key):
    base_key = jax.random.fold_in(key, 11)
    order = jax.random.permutation(jax.random.fold_in(base_key, 1), SLOTS)
    extra = jax.random.randint(jax.random.fold_in(base_key, 2), (SLOTS - PRIM,), 0, PRIM)
    listed = jnp.concatenate((jnp.arange(PRIM, dtype=jnp.int32), extra.astype(jnp.int32)))
    return listed[order].astype(jnp.int32)


def master_from(key):
    values = jax.random.normal(jax.random.fold_in(key, 21), (PRIM, FF, D), jnp.float32)
    return values * FF ** (-0.5)


def draw_plan(key, part):
    return plan_from(key)


def draw_master(key, part):
    return master_from(key)


def draw_down_weight(key, part):
    return master_from(key)[plan_from(key)].astype(jnp.bfloat16)


def draw_gate_weight(key, part):
    values = jax.random.normal(jax.random.fold_in(key, 31), (PRIM, D, FF), jnp.float32) * D ** (-0.5)
    return values[plan_from(key)].astype(jnp.bfloat16)


def draw_up_weight(key, part):
    values = jax.random.normal(jax.random.fold_in(key, 32), (PRIM, D, FF), jnp.float32) * D ** (-0.5)
    return values[plan_from(key)].astype(jnp.bfloat16)


def level_of(rng, extent, shards, smallest, largest):
    def one(dim, parts):
        steps = jax.random.uniform(jax.random.fold_in(jax.random.fold_in(rng, 6), dim), (parts,), jnp.float32, smallest / len(shards), largest / len(shards))
        return jnp.repeat(jnp.exp(steps), extent[dim] // parts).reshape((-1,) + (1,) * (len(extent) - dim - 1))

    gain = one(*shards[0])
    for cut in shards[1:]:
        gain = gain * one(*cut)
    return gain


def assign_block(own_key, own, number, rows, number_of, top, most, lean):
    order = jax.random.permutation(own_key, number_of)
    heavy_load, common = portions_of(number_of, rows * top, most, lean, True), portions_of(number_of, rows * top, most, lean, False)
    places = jnp.arange(number_of)

    def named(sizes, offset_by):
        used = int((sizes > 0).sum())
        fixed = max(1, used // 4)
        shifted = fixed + (places - fixed + offset_by * (used - fixed)) % max(1, number_of - fixed)
        return jnp.zeros((number_of,), jnp.int32).at[order[jnp.where(places < fixed, places, shifted)]].set(jnp.asarray(sizes, jnp.int32))

    sizes = jnp.where(number % 4 == 0, named(heavy_load, number // 4), named(common, number - number // 4 - 1))
    mixed = jax.random.permutation(jax.random.fold_in(own, 3), number_of)
    giver, receiver = mixed[0:number_of // 2 * 2:2], mixed[1:number_of // 2 * 2:2]
    margin = jnp.minimum(sizes[giver] - 1, most - sizes[receiver]) // 2
    margin = jnp.where((giver == order[0]) | (receiver == order[0]) | (sizes[receiver] == 0), 0, jnp.maximum(margin, 0))
    shifted = jax.random.randint(jax.random.fold_in(own, 4), (number_of // 2,), 0, 1 << 20) % (margin + 1)
    sizes = sizes.at[giver].add(-shifted).at[receiver].add(shifted)
    labels = jnp.searchsorted(jnp.cumsum(sizes), jnp.arange(rows * top), side="right").astype(jnp.int32)
    grid = labels.reshape(top, rows).T
    grid = grid[jax.random.permutation(jax.random.fold_in(own, 1), rows)]
    offset_by = jax.random.randint(jax.random.fold_in(own, 2), (rows, 1), 0, top)
    return jnp.take_along_axis(grid, (jnp.arange(top)[None, :] + offset_by) % top, axis=1)


def portions_of(amount, total, most, lean, full):
    loads = [(1 << 20) // math.isqrt(standing ** lean) + 1 for standing in range(1, amount + 1)]
    largest = most if full else min(most, max(-(-total // amount), total * loads[0] // sum(loads)))
    least = 1 if total - largest >= amount - 1 else 0
    given, spare = [largest] + [least] * (amount - 1), total - largest - least * (amount - 1)
    while spare > 0:
        candidates = [i for i in range(1, amount) if given[i] < largest] or [i for i in range(1, amount) if given[i] < most]
        mass, remaining = sum([loads[i] for i in candidates]), spare
        for i in candidates:
            more = min(most - given[i], max(1, remaining * loads[i] // mass), spare)
            given[i] = given[i] + more
            spare = spare - more
    return np.array(given)


def centred(own_key, dims, spread, most, pieces=(), kind=jnp.bfloat16):
    entries = spread * jax.random.normal(own_key, dims, jnp.float32)
    if pieces:
        entries = entries * level_of(own_key, dims, pieces, -0.22, 0.18)
    return jnp.clip(entries, -most, most).astype(kind)


def setup_inputs(seed: int = 0) -> dict:
    arg_keys = jax.random.split(jax.random.key(seed), 11)
    tokens = centred(arg_keys[0], (TOKENS, D), 1.0, 6.0, ((0, 32),))
    out_grad = centred(arg_keys[1], (TOKENS, D), 1.0, 6.0, ((0, 32),))
    routing_keys = jax.random.split(jax.random.fold_in(arg_keys[2], 1), TOKENS // TOK_DEV)
    routing_turns = jax.random.permutation(jax.random.fold_in(arg_keys[2], 3), TOKENS // TOK_DEV)
    routing = jax.vmap(lambda own, number: assign_block(jax.random.fold_in(arg_keys[2], 2), own, number, TOK_DEV, SLOTS, 1, CAP, 2))(routing_keys, routing_turns).reshape((TOKENS, 1))
    plan = draw_plan(jax.random.fold_in(arg_keys[10], 71), 0)
    gate_weight = draw_gate_weight(jax.random.fold_in(arg_keys[10], 71), 0)
    up_weight = draw_up_weight(jax.random.fold_in(arg_keys[10], 71), 0)
    down_weight = draw_down_weight(jax.random.fold_in(arg_keys[10], 71), 0)
    master = draw_master(jax.random.fold_in(arg_keys[10], 71), 0)
    moment = centred(arg_keys[8], (PRIM, FF, D), 4.0, 24.0, ((1, 32),), jnp.float32)
    second = jnp.clip(jnp.exp(math.log(400.0) - 5.9914645 * jax.random.uniform(arg_keys[9], (PRIM, FF, D), jnp.float32) ** level_of(arg_keys[9], (PRIM, FF, D), ((1, 32),), -0.2, 0.2)), 1.0, 400.0)
    return dict(tokens=tokens, out_grad=out_grad, routing=routing, plan=plan, gate_weight=gate_weight, up_weight=up_weight, down_weight=down_weight, master=master, moment=moment, second=second)


def adam_update(folded, master, moment, second):
    new_moment = 0.9 * moment + 0.1 * folded
    new_second = 0.95 * second + 0.05 * folded * folded
    first_hat = new_moment / (1.0 - 0.9 ** 10)
    second_hat = new_second / (1.0 - 0.95 ** 10)
    new_master = master - 0.01 * (first_hat / (jnp.sqrt(second_hat) + 1e-08) + 0.1 * master)
    return (new_master, new_moment, new_second)

def reference(tokens, out_grad, routing, plan, gate_weight, up_weight, down_weight, master, moment, second):
    sources = N_EXPERT * N_SLOT
    route = routing[:, 0].reshape(sources, TOK_DEV)
    onehot = (route[:, :, None] == jnp.arange(SLOTS, dtype=jnp.int32)[None, None, :]).astype(jnp.int32)
    rank = lax.optimization_barrier(jnp.sum(jnp.cumsum(onehot, axis=1) * onehot, axis=2)) - 1
    anchor = jnp.arange(sources, dtype=jnp.int32)[:, None]
    position = (route * (sources * CAP) + anchor * CAP + rank).reshape(-1).astype(jnp.int32)
    total = SLOTS * sources * CAP
    x_buffer = jnp.zeros((total, D), jnp.bfloat16).at[position].set(tokens).reshape(SLOTS, sources * CAP, D)
    g_buffer = jnp.zeros((total, D), jnp.bfloat16).at[position].set(out_grad).reshape(SLOTS, sources * CAP, D)

    def one_slot(items):
        x_rows, g_rows, w_gate, w_up, w_down = items
        gate = jnp.dot(x_rows, w_gate, preferred_element_type=jnp.float32)
        up = jnp.dot(x_rows, w_up, preferred_element_type=jnp.float32)
        sig = jax.nn.sigmoid(gate)
        silu_gate = gate * sig
        hidden = (silu_gate * up).astype(jnp.bfloat16)
        d_hidden = jnp.dot(g_rows, w_down.T, preferred_element_type=jnp.float32)
        d_gate = (d_hidden * up * sig * (1.0 + gate * (1.0 - sig))).astype(jnp.bfloat16)
        d_up = (d_hidden * silu_gate).astype(jnp.bfloat16)
        d_input = jnp.dot(d_gate, w_gate.T, preferred_element_type=jnp.float32)
        d_input = d_input + jnp.dot(d_up, w_up.T, preferred_element_type=jnp.float32)
        grad = jnp.dot(hidden.T, g_rows, preferred_element_type=jnp.float32)
        return (d_input.astype(jnp.bfloat16), grad)
    dx_buffer, grads = lax.map(one_slot, (x_buffer, g_buffer, gate_weight, up_weight, down_weight))
    token_grad = dx_buffer.reshape(total, D)[position]
    select = (plan[None, :] == jnp.arange(PRIM, dtype=jnp.int32)[:, None]).astype(jnp.float32)
    folded = jnp.einsum('ps,sfd->pfd', select, grads, precision=lax.Precision.HIGHEST)
    new_master, new_moment, new_second = adam_update(folded, master, moment, second)
    new_down = new_master.astype(jnp.bfloat16)[plan]
    return (token_grad, new_master, new_moment, new_second, new_down)
```

```python
import functools

import jax
import jax.numpy as jnp
from jax import lax
from jax.experimental import pallas as pl
from jax.experimental.pallas import tpu as pltpu
from jax.sharding import PartitionSpec as P

BF16 = jnp.bfloat16
F32 = jnp.float32
NT = (((1,), (1,)), ((), ()))
TN = (((0,), (0,)), ((), ()))
NN = (((1,), (0,)), ((), ()))
COLUMNS = 512


def dot(a, b, dims):
    return lax.dot_general(a, b, dims, preferred_element_type=F32)


def call(kernel, outs, args, scratch=(), smem=(), name=None, mib=40, flops=0):
    moved = sum(a.size * a.dtype.itemsize for a in args) + sum(
        o.size * o.dtype.itemsize for o in outs
    )
    return pl.pallas_call(
        kernel,
        out_shape=tuple(outs),
        in_specs=[
            pl.BlockSpec(memory_space=pltpu.SMEM if i in smem else pltpu.VMEM)
            for i in range(len(args))
        ],
        out_specs=tuple(pl.BlockSpec(memory_space=pltpu.VMEM) for _ in outs),
        scratch_shapes=list(scratch),
        compiler_params=pltpu.CompilerParams(vmem_limit_bytes=mib * 2**20),
        cost_estimate=pl.CostEstimate(flops=flops, bytes_accessed=moved, transcendentals=0),
        name=name,
    )(*args)


def columns(width):
    step = min(COLUMNS, width)
    return [slice(c, c + step) for c in range(0, width, step)]


def pack_kernel(n, capacity, joint, r_ref, x_ref, g_ref, place_ref, *outs):
    e = lax.axis_index("expert")
    owned, width = x_ref.shape
    rel = r_ref[...] ^ e
    lane = lax.broadcasted_iota(jnp.int32, (owned, n), 1)
    match = (rel == lane).astype(F32)
    lower = lax.broadcasted_iota(jnp.int32, (owned, owned), 0) >= lax.broadcasted_iota(
        jnp.int32, (owned, owned), 1
    )
    count = dot(lower.astype(BF16), match.astype(BF16), NN)
    pos = jnp.sum(match * (count - 1.0 + (lane * capacity).astype(F32)), axis=1, keepdims=True)
    spot = lax.broadcasted_iota(jnp.int32, (owned, n * capacity), 1)
    place = (pos.astype(jnp.int32) == spot).astype(BF16)
    place_ref[...] = place
    for cols in columns(width):
        for half, ref in enumerate((x_ref, g_ref)):
            packed = dot(place, ref[:, cols], TN).astype(BF16)
            if joint:
                for d in range(n):
                    outs[d][half * capacity : (half + 1) * capacity, cols] = packed[
                        d * capacity : (d + 1) * capacity
                    ]
            else:
                outs[half][:, cols] = packed


def turn_kernel(gate_ref, up_ref, out_ref):
    part = gate_ref.shape[2]
    out_ref[:part] = gate_ref[0].T
    out_ref[part:] = up_ref[0].T


def halves(blocks, half):
    parts = []
    for ref in blocks:
        rows = ref.shape[0] // 2
        parts.append(ref[half * rows : (half + 1) * rows])
    return parts[0] if len(parts) == 1 else jnp.concatenate(parts, axis=0)


def hidden_kernel(nb, m, *refs):
    blocks, weights = refs[:nb], refs[nb : nb + m]
    hidden_ref, a_ref, b_ref = refs[nb + m :]
    x = halves(blocks, 0)
    part = weights[0].shape[0] // 2
    for r in range(m):
        gate = dot(weights[r][:part], x, NT)
        up = dot(weights[r][part:], x, NT)
        sig = jax.nn.sigmoid(gate)
        silu = gate * sig
        hidden_ref[r] = (silu * up).astype(BF16)
        a_ref[r] = up * sig * (1.0 + gate * (1.0 - sig))
        b_ref[r] = silu


def grad_kernel(nb, m, *refs):
    blocks, hidden_ref = refs[:nb], refs[nb]
    send_ref, keep_ref = refs[nb + 1 :]
    part = hidden_ref.shape[1]
    g = halves(blocks, 1)
    for r in range(m):
        rows = slice(r // 2 * part, (r // 2 + 1) * part)
        for cols in columns(g.shape[1]):
            value = dot(hidden_ref[r], g[:, cols], NN)
            if r % 2:
                send_ref[rows, cols] = value.astype(BF16)
            else:
                keep_ref[rows, cols] = value


def back_kernel(nb, m, *refs):
    blocks, weights, down = refs[:nb], refs[nb : nb + m], refs[nb + m : nb + 2 * m]
    a_ref, b_ref = refs[nb + 2 * m : nb + 2 * m + 2]
    outs, (total, turned) = refs[nb + 2 * m + 2 : -2], refs[-2:]
    g = halves(blocks, 1)
    part = down[0].shape[0]
    for r in range(m):
        dh = dot(down[r][...], g, NT)
        turned[r, :part] = (dh * a_ref[r]).astype(BF16)
        turned[r, part:] = (dh * b_ref[r]).astype(BF16)
    for cols in columns(g.shape[1]):
        acc = dot(turned[0], weights[0][:, cols], TN)
        for r in range(1, m):
            acc = acc + dot(turned[r], weights[r][:, cols], TN)
        acc = acc.astype(BF16)
        start = 0
        for out in outs:
            out[:, cols] = acc[start : start + out.shape[0]]
            start += out.shape[0]


def add_kernel(keep_ref, got_ref, first_ref, *rest):
    part = first_ref.shape[0]
    first_ref[...] = keep_ref[:part] + got_ref[:part].astype(F32)
    for i, out in enumerate(rest, 1):
        rows = slice(i * part, (i + 1) * part)
        out[...] = (keep_ref[rows] + got_ref[rows].astype(F32)).astype(BF16)


def cut_kernel(count, first_ref, *refs):
    got, outs, sums = refs[:count], refs[count:-1], refs[-1]
    e = lax.axis_index("expert")
    total = first_ref[...]
    for ref in got:
        total = total + ref[...].astype(F32)
    if len(outs) == 1:
        outs[0][...] = total.astype(BF16)
        return
    sums[...] = total
    rows = outs[0].shape[0]
    for d, out in enumerate(outs):
        out[...] = sums[pl.ds(pl.multiple_of((e ^ d) * rows, 8), rows)].astype(BF16)


def adam_kernel(n, pieces_in, *refs):
    plan_ref = refs[0]
    pieces, (master_ref, moment_ref, second_ref) = refs[1 : 1 + pieces_in], refs[
        1 + pieces_in : 4 + pieces_in
    ]
    new_master, new_moment, new_second = refs[4 + pieces_in : 7 + pieces_in]
    outs, folded = refs[7 + pieces_in : -1], refs[-1]
    e = lax.axis_index("expert")
    primaries = master_ref.shape[0]
    folded[...] = jnp.zeros_like(folded)
    for d in range(n):
        p = plan_ref[e ^ d]
        piece = pieces[0][d] if pieces_in == 1 else pieces[d][...]
        folded[p] = folded[p] + piece.astype(F32)
    for p in range(primaries):
        total = folded[p]
        moment = 0.9 * moment_ref[p] + 0.1 * total
        second = 0.95 * second_ref[p] + 0.05 * total * total
        new_moment[p] = moment
        new_second[p] = second
        master = master_ref[p]
        first_hat = moment / (1.0 - 0.9**10)
        second_hat = second / (1.0 - 0.95**10)
        new_master[p] = master - 0.01 * (
            first_hat / (jnp.sqrt(second_hat) + 1e-08) + 0.1 * master
        )
    for d in range(n):
        row = new_master[plan_ref[e ^ d]].astype(BF16)
        if len(outs) == 1:
            outs[0][d] = row
        else:
            outs[d][...] = row


def unpack_kernel(place_ref, *refs):
    blocks, out_ref = refs[:-1], refs[-1]
    place = place_ref[...]
    for cols in columns(out_ref.shape[1]):
        parts = [b[:, cols] for b in blocks]
        rows = parts[0] if len(parts) == 1 else jnp.concatenate(parts, axis=0)
        out_ref[:, cols] = dot(place, rows, NN).astype(BF16)


def swap(x, axis, mask):
    size = lax.axis_size(axis)
    return lax.ppermute(x, axis, [(i, i ^ mask) for i in range(size)])


def order(n):
    return sorted(range(1, n), key=lambda d: -(d >> 1))


def exchange(blocks):
    n = len(blocks)
    got = {0: blocks[0]}
    for d in order(n):
        got[d] = swap(blocks[d], "expert", d)
    return [got[d] for d in range(n)]


def exchange_whole(x):
    n = x.shape[0]
    turn = jnp.arange(n, dtype=jnp.int32) ^ lax.axis_index("expert")
    x = jnp.take(x, turn, axis=0)
    x = lax.all_to_all(x, "expert", split_axis=0, concat_axis=0, tiled=True)
    return jnp.take(x, turn, axis=0)


def gather_slot(x):
    m = lax.axis_size("slot")
    have = {0: x}
    mask = m // 2
    while mask:
        for r in sorted(have):
            have[r | mask] = swap(have[r], "slot", mask)
        mask //= 2
    return [have[r] for r in range(m)]


def body(
    tokens, out_grad, routing, plan, gate_weight, up_weight, down_weight, master, moment, second
):
    n, m = lax.axis_size("expert"), lax.axis_size("slot")
    owned, width = tokens.shape
    capacity = 2 * owned // n
    part = down_weight.shape[1]
    rows = n * capacity
    few = capacity % 16 == 0
    turn = jnp.arange(n, dtype=jnp.int32) ^ lax.axis_index("expert")
    shape = jax.ShapeDtypeStruct

    outs = [shape((owned, rows), BF16)]
    outs += [shape((2 * capacity, width), BF16)] * n if few else [shape((rows, width), BF16)] * 2
    place, *packed = call(
        functools.partial(pack_kernel, n, capacity, few),
        outs,
        (routing, tokens, out_grad),
        name="pack_rows",
        flops=4 * owned * rows * width,
    )
    (joined,) = call(
        turn_kernel, [shape((2 * part, width), BF16)], (gate_weight, up_weight), name="turn_weights"
    )
    if few:
        blocks = exchange(packed)
    else:
        x, g = (
            exchange_whole(p.reshape(n, capacity, width)).reshape(rows, width) for p in packed
        )
        blocks = [jnp.concatenate((x, g), axis=0)]
    nb = len(blocks)
    joined = gather_slot(joined)
    down = gather_slot(down_weight[0])

    hidden, a, b = call(
        functools.partial(hidden_kernel, nb, m),
        [shape((m, part, rows), BF16), shape((m, part, rows), F32), shape((m, part, rows), F32)],
        (*blocks, *joined),
        name="hidden_units",
        flops=4 * rows * width * part * m,
    )
    send, keep = call(
        functools.partial(grad_kernel, nb, m),
        [shape((m // 2 * part, width), BF16), shape((m // 2 * part, width), F32)],
        (*blocks, hidden),
        name="down_gradient",
        flops=2 * rows * width * part * m,
    )
    dx = call(
        functools.partial(back_kernel, nb, m),
        [shape((r.shape[0] // 2, width), BF16) for r in blocks],
        (*blocks, *joined, *down, a, b),
        scratch=[pltpu.VMEM((8, 128), F32), pltpu.VMEM((m, 2 * part, rows), BF16)],
        name="input_gradient",
        flops=6 * rows * width * part * m,
    )
    got = swap(send, "slot", 1)
    first, *rest = call(
        add_kernel,
        [shape((part, width), F32)] + [shape((part, width), BF16)] * (m // 2 - 1),
        (keep, got),
        name="add_pair",
    )
    if few:
        returned = exchange(dx)
    else:
        returned = [exchange_whole(dx[0].reshape(n, capacity, width)).reshape(rows, width)]
    rest = [swap(r, "slot", 2 * i) for i, r in enumerate(rest, 1)]
    owner = part // n
    pieces = call(
        functools.partial(cut_kernel, len(rest)),
        [shape((owner, width), BF16)] * n if few else [shape((part, width), BF16)],
        (first, *rest),
        scratch=[pltpu.VMEM((part, width), F32)],
        name="cut_gradient",
    )
    if few:
        arrived = exchange(pieces)
    else:
        arrived = [exchange_whole(jnp.take(pieces[0].reshape(n, owner, width), turn, axis=0))]
    new_master, new_moment, new_second, *outgoing = call(
        functools.partial(adam_kernel, n, len(arrived)),
        [shape(master.shape, F32)] * 3
        + ([shape((owner, width), BF16)] * n if few else [shape((n, owner, width), BF16)]),
        (plan, *arrived, master, moment, second),
        scratch=[pltpu.VMEM(master.shape, F32)],
        smem=(0,),
        name="adam",
    )
    (token_grad,) = call(
        unpack_kernel,
        [shape((owned, width), BF16)],
        (place, *returned),
        name="unpack_rows",
        flops=2 * owned * rows * width,
    )
    if few:
        fresh = jnp.take(jnp.stack(exchange(outgoing)), turn, axis=0)
    else:
        fresh = exchange_whole(outgoing[0])
    return (token_grad, new_master, new_moment, new_second, fresh.reshape(1, part, width))


def solution(mesh):
    rows, state = P(("expert", "slot"), None), P(None, ("slot", "expert"), None)
    split, held = P("expert", None, "slot"), P("expert", "slot", None)
    return jax.shard_map(
        body,
        mesh=mesh,
        in_specs=(rows, rows, rows, P(), split, split, held, state, state, state),
        out_specs=(rows, state, state, state, held),
        check_vma=False,
    )
```

```python
import functools

import jax
import jax.numpy as jnp
from jax import lax
from jax.experimental import pallas as pl
from jax.experimental.pallas import tpu as pltpu
from jax.sharding import PartitionSpec as P

BF16 = jnp.bfloat16
F32 = jnp.float32
NT = (((1,), (1,)), ((), ()))
TN = (((0,), (0,)), ((), ()))
NN = (((1,), (0,)), ((), ()))
COLUMNS = 512


def dot(a, b, dims):
    return lax.dot_general(a, b, dims, preferred_element_type=F32)


def call(
    kernel, outs, args, scratch=(), smem=(), far=(), far_out=(), name=None, mib=40, flops=0
):
    moved = sum(a.size * a.dtype.itemsize for a in args) + sum(
        o.size * o.dtype.itemsize for o in outs
    )
    return pl.pallas_call(
        kernel,
        out_shape=tuple(outs),
        in_specs=[
            pl.BlockSpec(
                memory_space=pltpu.SMEM if i in smem else pl.ANY if i in far else pltpu.VMEM
            )
            for i in range(len(args))
        ],
        out_specs=tuple(
            pl.BlockSpec(memory_space=pl.ANY if i in far_out else pltpu.VMEM)
            for i in range(len(outs))
        ),
        scratch_shapes=list(scratch),
        compiler_params=pltpu.CompilerParams(vmem_limit_bytes=mib * 2**20),
        cost_estimate=pl.CostEstimate(flops=flops, bytes_accessed=moved, transcendentals=0),
        name=name,
    )(*args)


def columns(width):
    step = min(COLUMNS, width)
    return [slice(c, c + step) for c in range(0, width, step)]


def pack_kernel(
    n, capacity, joint, r_ref, x_ref, g_ref, gate_ref, up_ref, place_ref, joined_ref, *rest
):
    outs, sem = rest[:-1], rest[-1]
    part = gate_ref.shape[0]
    copies = [
        pltpu.make_async_copy(ref, joined_ref.at[i * part : (i + 1) * part], sem.at[i])
        for i, ref in enumerate((gate_ref, up_ref))
    ]
    for copy in copies:
        copy.start()
    e = lax.axis_index("expert")
    owned, width = x_ref.shape
    rel = r_ref[...] ^ e
    lane = lax.broadcasted_iota(jnp.int32, (owned, n), 1)
    match = (rel == lane).astype(F32)
    lower = lax.broadcasted_iota(jnp.int32, (owned, owned), 0) >= lax.broadcasted_iota(
        jnp.int32, (owned, owned), 1
    )
    count = dot(lower.astype(BF16), match.astype(BF16), NN)
    pos = jnp.sum(match * (count - 1.0 + (lane * capacity).astype(F32)), axis=1, keepdims=True)
    spot = lax.broadcasted_iota(jnp.int32, (owned, n * capacity), 1)
    place = (pos.astype(jnp.int32) == spot).astype(BF16)
    place_ref[...] = place
    for cols in columns(width):
        for half, ref in enumerate((x_ref, g_ref)):
            packed = dot(place, ref[:, cols], TN).astype(BF16)
            if joint:
                for d in range(n):
                    outs[d][half * capacity : (half + 1) * capacity, cols] = packed[
                        d * capacity : (d + 1) * capacity
                    ]
            else:
                outs[half][:, cols] = packed
    for copy in copies:
        copy.wait()


def halves(blocks, half):
    parts = []
    for ref in blocks:
        rows = ref.shape[0] // 2
        parts.append(ref[half * rows : (half + 1) * rows])
    return parts[0] if len(parts) == 1 else jnp.concatenate(parts, axis=0)


def fetch(pairs, sem):
    copies = [pltpu.make_async_copy(src, dst, sem.at[i]) for i, (src, dst) in enumerate(pairs)]
    for copy in copies:
        copy.start()
    return copies


def hidden_kernel(nb, m, *refs):
    blocks, weights = refs[:nb], refs[nb : nb + m]
    send_ref, keep_ref, a_ref, b_ref, held, hidden, sem = refs[nb + m :]
    copies = fetch([(w, held.at[r]) for r, w in enumerate(weights)], sem)
    x = halves(blocks, 0)
    part = weights[0].shape[0] // 2
    for r in range(m):
        copies[r].wait()
        gate = dot(held[r, :part], x, NT)
        up = dot(held[r, part:], x, NT)
        sig = jax.nn.sigmoid(gate)
        silu = gate * sig
        hidden[r] = (silu * up).astype(BF16)
        a_ref[r] = up * sig * (1.0 + gate * (1.0 - sig))
        b_ref[r] = silu
    g = halves(blocks, 1)
    for r in range(m):
        rows = slice(r // 2 * part, (r // 2 + 1) * part)
        for cols in columns(g.shape[1]):
            value = dot(hidden[r], g[:, cols], NN)
            if r % 2:
                send_ref[rows, cols] = value.astype(BF16)
            else:
                keep_ref[rows, cols] = value


def back_kernel(nb, m, *refs):
    blocks, weights, down = refs[:nb], refs[nb : nb + m], refs[nb + m : nb + 2 * m]
    a_ref, b_ref = refs[nb + 2 * m : nb + 2 * m + 2]
    outs, (held, low, turned, sem) = refs[nb + 2 * m + 2 : -4], refs[-4:]
    pairs = [(d, low.at[r]) for r, d in enumerate(down)]
    copies = fetch(pairs + [(w, held.at[r]) for r, w in enumerate(weights)], sem)
    g = halves(blocks, 1)
    part = down[0].shape[0]
    for r in range(m):
        copies[r].wait()
        dh = dot(low[r], g, NT)
        turned[r, :part] = (dh * a_ref[r]).astype(BF16)
        turned[r, part:] = (dh * b_ref[r]).astype(BF16)
    for r in range(m):
        copies[m + r].wait()
    for cols in columns(g.shape[1]):
        acc = dot(turned[0], held[0, :, cols], TN)
        for r in range(1, m):
            acc = acc + dot(turned[r], held[r, :, cols], TN)
        acc = acc.astype(BF16)
        start = 0
        for out in outs:
            out[:, cols] = acc[start : start + out.shape[0]]
            start += out.shape[0]


def add_kernel(keep_ref, got_ref, first_ref, *rest):
    part = first_ref.shape[0]
    first_ref[...] = keep_ref[:part] + got_ref[:part].astype(F32)
    for i, out in enumerate(rest, 1):
        rows = slice(i * part, (i + 1) * part)
        out[...] = (keep_ref[rows] + got_ref[rows].astype(F32)).astype(BF16)


def cut_kernel(count, first_ref, *refs):
    got, outs, sums = refs[:count], refs[count:-1], refs[-1]
    e = lax.axis_index("expert")
    total = first_ref[...]
    for ref in got:
        total = total + ref[...].astype(F32)
    if len(outs) == 1:
        outs[0][...] = total.astype(BF16)
        return
    sums[...] = total
    rows = outs[0].shape[0]
    for d, out in enumerate(outs):
        out[...] = sums[pl.ds(pl.multiple_of((e ^ d) * rows, 8), rows)].astype(BF16)


def adam_kernel(n, pieces_in, *refs):
    plan_ref = refs[0]
    pieces, (master_ref, moment_ref, second_ref) = refs[1 : 1 + pieces_in], refs[
        1 + pieces_in : 4 + pieces_in
    ]
    new_master, new_moment, new_second = refs[4 + pieces_in : 7 + pieces_in]
    outs, folded = refs[7 + pieces_in : -1], refs[-1]
    e = lax.axis_index("expert")
    primaries = master_ref.shape[0]
    folded[...] = jnp.zeros_like(folded)
    for d in range(n):
        p = plan_ref[e ^ d]
        piece = pieces[0][d] if pieces_in == 1 else pieces[d][...]
        folded[p] = folded[p] + piece.astype(F32)
    for p in range(primaries):
        total = folded[p]
        moment = 0.9 * moment_ref[p] + 0.1 * total
        second = 0.95 * second_ref[p] + 0.05 * total * total
        new_moment[p] = moment
        new_second[p] = second
        master = master_ref[p]
        first_hat = moment / (1.0 - 0.9**10)
        second_hat = second / (1.0 - 0.95**10)
        new_master[p] = master - 0.01 * (
            first_hat / (jnp.sqrt(second_hat) + 1e-08) + 0.1 * master
        )
    for d in range(n):
        row = new_master[plan_ref[e ^ d]].astype(BF16)
        if len(outs) == 1:
            outs[0][d] = row
        else:
            outs[d][...] = row


def unpack_kernel(place_ref, *refs):
    blocks, out_ref = refs[:-1], refs[-1]
    place = place_ref[...]
    for cols in columns(out_ref.shape[1]):
        parts = [b[:, cols] for b in blocks]
        rows = parts[0] if len(parts) == 1 else jnp.concatenate(parts, axis=0)
        out_ref[:, cols] = dot(place, rows, NN).astype(BF16)


def order_kernel(n, *refs):
    e = lax.axis_index("expert")
    for d in range(n):
        refs[n][e ^ d] = refs[d][...]


def swap(x, axis, mask):
    size = lax.axis_size(axis)
    return lax.ppermute(x, axis, [(i, i ^ mask) for i in range(size)])


def order(n):
    return sorted(range(1, n), key=lambda d: -(d >> 1))


def exchange(blocks):
    n = len(blocks)
    got = {0: blocks[0]}
    for d in order(n):
        got[d] = swap(blocks[d], "expert", d)
    return [got[d] for d in range(n)]


def exchange_whole(x):
    n = x.shape[0]
    turn = jnp.arange(n, dtype=jnp.int32) ^ lax.axis_index("expert")
    x = jnp.take(x, turn, axis=0)
    x = lax.all_to_all(x, "expert", split_axis=0, concat_axis=0, tiled=True)
    return jnp.take(x, turn, axis=0)


def far_steps(m):
    masks = [1 << i for i in range(m.bit_length() - 1)]
    return masks[:0:-1]


def gather_far(x, m):
    have = {0: x}
    for mask in far_steps(m):
        for r in sorted(have):
            have[r | mask] = swap(have[r], "slot", mask)
    return have


def gather_near(have, m):
    have = dict(have)
    for r in sorted(have):
        have[r | 1] = swap(have[r], "slot", 1)
    return [have[r] for r in range(m)]


def after(x, *others):
    return lax.optimization_barrier((x, *others))


def body(
    tokens, out_grad, routing, plan, gate_weight, up_weight, down_weight, master, moment, second
):
    n, m = lax.axis_size("expert"), lax.axis_size("slot")
    owned, width = tokens.shape
    capacity = 2 * owned // n
    part = down_weight.shape[1]
    rows = n * capacity
    few = capacity % 16 == 0
    turn = jnp.arange(n, dtype=jnp.int32) ^ lax.axis_index("expert")
    shape = jax.ShapeDtypeStruct

    outs = [shape((owned, rows), BF16), shape((2 * part, width), BF16)]
    outs += [shape((2 * capacity, width), BF16)] * n if few else [shape((rows, width), BF16)] * 2
    gate_rows, up_rows = (jnp.swapaxes(w, 1, 2)[0] for w in (gate_weight, up_weight))
    place, joined, *packed = call(
        functools.partial(pack_kernel, n, capacity, few),
        outs,
        (routing, tokens, out_grad, gate_rows, up_rows),
        scratch=[pltpu.SemaphoreType.DMA((2,))],
        far=(3, 4),
        far_out=(1,),
        name="pack_rows",
        flops=4 * owned * rows * width,
    )
    joined = gather_far(joined, m)
    if few:
        blocks = exchange(packed)
    else:
        x, g = (
            exchange_whole(p.reshape(n, capacity, width)).reshape(rows, width) for p in packed
        )
        blocks = [jnp.concatenate((x, g), axis=0)]
    nb = len(blocks)
    down, blocks[nb // 2] = after(down_weight[0], blocks[nb // 2])
    down = gather_far(down, m)
    blocks, joined = lax.optimization_barrier((blocks, joined))
    joined = gather_near(joined, m)

    send, keep, a, b = call(
        functools.partial(hidden_kernel, nb, m),
        [
            shape((m // 2 * part, width), BF16),
            shape((m // 2 * part, width), F32),
            shape((m, part, rows), F32),
            shape((m, part, rows), F32),
        ],
        (*blocks, *joined),
        scratch=[
            pltpu.VMEM((m, 2 * part, width), BF16),
            pltpu.VMEM((m, part, rows), BF16),
            pltpu.SemaphoreType.DMA((m,)),
        ],
        far=range(nb, nb + m),
        name="hidden_units",
        flops=6 * rows * width * part * m,
    )
    send, down = lax.optimization_barrier((send, down))
    got = swap(send, "slot", 1)
    down = gather_near(down, m)
    dx = call(
        functools.partial(back_kernel, nb, m),
        [shape((r.shape[0] // 2, width), BF16) for r in blocks],
        (*blocks, *joined, *down, a, b),
        scratch=[
            pltpu.VMEM((m, 2 * part, width), BF16),
            pltpu.VMEM((m, part, width), BF16),
            pltpu.VMEM((m, 2 * part, rows), BF16),
            pltpu.SemaphoreType.DMA((2 * m,)),
        ],
        far=range(nb, nb + 2 * m),
        name="input_gradient",
        flops=6 * rows * width * part * m,
    )
    first, *rest = call(
        add_kernel,
        [shape((part, width), F32)] + [shape((part, width), BF16)] * (m // 2 - 1),
        (keep, got),
        name="add_pair",
    )
    if few:
        returned = exchange(dx)
    else:
        returned = [exchange_whole(dx[0].reshape(n, capacity, width)).reshape(rows, width)]
    rest = [swap(r, "slot", 2 * i) for i, r in enumerate(rest, 1)]
    owner = part // n
    pieces = call(
        functools.partial(cut_kernel, len(rest)),
        [shape((owner, width), BF16)] * n if few else [shape((part, width), BF16)],
        (first, *rest),
        scratch=[pltpu.VMEM((part, width), F32)],
        name="cut_gradient",
    )
    if few:
        arrived = exchange(pieces)
    else:
        arrived = [exchange_whole(jnp.take(pieces[0].reshape(n, owner, width), turn, axis=0))]
    new_master, new_moment, new_second, *outgoing = call(
        functools.partial(adam_kernel, n, len(arrived)),
        [shape(master.shape, F32)] * 3
        + ([shape((owner, width), BF16)] * n if few else [shape((n, owner, width), BF16)]),
        (plan, *arrived, master, moment, second),
        scratch=[pltpu.VMEM(master.shape, F32)],
        smem=(0,),
        name="adam",
    )
    (token_grad,) = call(
        unpack_kernel,
        [shape((owned, width), BF16)],
        (place, *returned),
        name="unpack_rows",
        flops=2 * owned * rows * width,
    )
    if few:
        (fresh,) = call(
            functools.partial(order_kernel, n),
            [shape((n, owner, width), BF16)],
            exchange(outgoing),
            name="order_rows",
        )
    else:
        fresh = exchange_whole(outgoing[0])
    return (token_grad, new_master, new_moment, new_second, fresh.reshape(1, part, width))


def solution(mesh):
    rows, state = P(("expert", "slot"), None), P(None, ("slot", "expert"), None)
    split, held = P("expert", None, "slot"), P("expert", "slot", None)
    return jax.shard_map(
        body,
        mesh=mesh,
        in_specs=(rows, rows, rows, P(), split, split, held, state, state, state),
        out_specs=(rows, state, state, state, held),
        check_vma=False,
    )
```

```python
import functools

import jax
import jax.numpy as jnp
from jax import lax
from jax.experimental import pallas as pl
from jax.experimental.pallas import tpu as pltpu
from jax.sharding import PartitionSpec as P

BF16 = jnp.bfloat16
F32 = jnp.float32
NT = (((1,), (1,)), ((), ()))
TN = (((0,), (0,)), ((), ()))
NN = (((1,), (0,)), ((), ()))
COLUMNS = 512
EARLY = 5


def dot(a, b, dims):
    return lax.dot_general(a, b, dims, preferred_element_type=F32)


def call(
    kernel, outs, args, scratch=(), smem=(), far=(), far_out=(), name=None, mib=40, flops=0
):
    moved = sum(a.size * a.dtype.itemsize for a in args) + sum(
        o.size * o.dtype.itemsize for o in outs
    )
    return pl.pallas_call(
        kernel,
        out_shape=tuple(outs),
        in_specs=[
            pl.BlockSpec(
                memory_space=pltpu.SMEM if i in smem else pl.ANY if i in far else pltpu.VMEM
            )
            for i in range(len(args))
        ],
        out_specs=tuple(
            pl.BlockSpec(memory_space=pl.ANY if i in far_out else pltpu.VMEM)
            for i in range(len(outs))
        ),
        scratch_shapes=list(scratch),
        compiler_params=pltpu.CompilerParams(vmem_limit_bytes=mib * 2**20),
        cost_estimate=pl.CostEstimate(flops=flops, bytes_accessed=moved, transcendentals=0),
        name=name,
    )(*args)


def columns(width):
    step = min(COLUMNS, width)
    return [slice(c, c + step) for c in range(0, width, step)]


def pack_kernel(n, capacity, joint, r_ref, x_ref, g_ref, *refs):
    weights, place_ref, joined_ref, outs = refs[:3], refs[3], refs[4], refs[5:-3]
    x_held, g_held, sem = refs[-3:]
    part = weights[0].shape[0]
    pairs = [(x_ref, x_held), (g_ref, g_held)]
    pairs += [(w, joined_ref.at[i * part : (i + 1) * part]) for i, w in enumerate(weights)]
    copies = [pltpu.make_async_copy(src, dst, sem.at[i]) for i, (src, dst) in enumerate(pairs)]
    for copy in copies:
        copy.start()
    e = lax.axis_index("expert")
    owned, width = x_ref.shape
    rel = r_ref[...] ^ e
    block = lax.broadcasted_iota(jnp.int32, (n, owned), 0)
    match = (rel == block).astype(F32)
    upper = lax.broadcasted_iota(jnp.int32, (owned, owned), 0) <= lax.broadcasted_iota(
        jnp.int32, (owned, owned), 1
    )
    count = dot(match.astype(BF16), upper.astype(BF16), NN)
    pos = jnp.sum(match * (count - 1.0 + (block * capacity).astype(F32)), axis=0, keepdims=True)
    spot = lax.broadcasted_iota(jnp.int32, (n * capacity, owned), 0)
    place = (pos.astype(jnp.int32) == spot).astype(BF16)
    place_ref[...] = place
    for half, held in enumerate((x_held, g_held)):
        copies[half].wait()
        for cols in columns(width):
            packed = dot(place, held[:, cols], NN).astype(BF16)
            if joint:
                for d in range(n):
                    outs[d][half * capacity : (half + 1) * capacity, cols] = packed[
                        d * capacity : (d + 1) * capacity
                    ]
            else:
                outs[half][:, cols] = packed
    for copy in copies[2:]:
        copy.wait()


def halves(blocks, half):
    parts = []
    for ref in blocks:
        rows = ref.shape[0] // 2
        parts.append(ref[half * rows : (half + 1) * rows])
    return parts[0] if len(parts) == 1 else jnp.concatenate(parts, axis=0)


def forward(weight, x):
    part = weight.shape[0] // 3
    both = dot(weight[: 2 * part], x, NT)
    gate, up = both[:part], both[part:]
    sig = jax.nn.sigmoid(gate)
    silu = gate * sig
    return (silu * up).astype(BF16), up * sig * (1.0 + gate * (1.0 - sig)), silu


def weight_gradient(hidden, g, send_ref, keep_ref):
    part = hidden.shape[1]
    for r in range(hidden.shape[0]):
        rows = slice(r // 2 * part, (r // 2 + 1) * part)
        for cols in columns(g.shape[1]):
            value = dot(hidden[r], g[:, cols], NN).astype(BF16)
            (send_ref if r % 2 else keep_ref)[rows, cols] = value


def turn(weight, g, a, b):
    part = weight.shape[0] // 3
    dh = dot(weight[2 * part :], g, NT)
    both = jnp.concatenate(((dh * a).astype(BF16), (dh * b).astype(BF16)), axis=0)
    return both.T


def input_gradient(turned, weights, cols):
    wide = weights[0].shape[0] // 3 * 2
    total = None
    for r, weight in enumerate(weights):
        term = dot(turned[:, r * wide : (r + 1) * wide], weight[:wide, cols], NN)
        total = term if total is None else total + term
    return total


def near_kernel(nb, nw, *refs):
    blocks, weights = refs[:nb], refs[nb : nb + nw]
    send_ref, keep_ref, partial_ref, hidden, turned = refs[nb + nw :]
    x, g = halves(blocks, 0), halves(blocks, 1)
    wide = weights[0].shape[0] // 3 * 2
    for r in range(nw):
        hidden[r], a, b = forward(weights[r], x)
        turned[:, r * wide : (r + 1) * wide] = turn(weights[r], g, a, b)
    weight_gradient(hidden, g, send_ref, keep_ref)
    for cols in columns(g.shape[1]):
        partial_ref[:, cols] = input_gradient(turned, weights, cols)


def hidden_kernel(nb, nw, *refs):
    blocks, weights = refs[:nb], refs[nb : nb + nw]
    send_ref, keep_ref, a_ref, b_ref, hidden = refs[nb + nw :]
    x, g = halves(blocks, 0), halves(blocks, 1)
    for r in range(nw):
        hidden[r], a_ref[r], b_ref[r] = forward(weights[r], x)
    weight_gradient(hidden, g, send_ref, keep_ref)


def back_kernel(nb, nw, *refs):
    blocks, weights = refs[:nb], refs[nb : nb + nw]
    a_ref, b_ref, partial_ref = refs[nb + nw : nb + nw + 3]
    outs, turned = refs[nb + nw + 3 : -1], refs[-1]
    g = halves(blocks, 1)
    wide = weights[0].shape[0] // 3 * 2
    for r in range(nw):
        turned[:, r * wide : (r + 1) * wide] = turn(weights[r], g, a_ref[r], b_ref[r])
    for cols in columns(g.shape[1]):
        total = (partial_ref[:, cols] + input_gradient(turned, weights, cols)).astype(BF16)
        start = 0
        for out in outs:
            out[:, cols] = total[start : start + out.shape[0]]
            start += out.shape[0]


def add_kernel(keep_ref, got_ref, *outs):
    part = outs[0].shape[0]
    for i, out in enumerate(outs):
        rows = slice(i * part, (i + 1) * part)
        out[...] = (keep_ref[rows].astype(F32) + got_ref[rows].astype(F32)).astype(BF16)


def cut_kernel(count, blocks, *refs):
    terms, outs, sums = refs[:count], refs[count:-1], refs[-1]
    e = lax.axis_index("expert")
    total = terms[0][...].astype(F32)
    for ref in terms[1:]:
        total = total + ref[...].astype(F32)
    if len(outs) == 1:
        outs[0][...] = total.astype(BF16)
        return
    sums[...] = total
    rows = outs[0].shape[0]
    for d, out in zip(blocks, outs, strict=True):
        out[...] = sums[pl.ds(pl.multiple_of((e ^ d) * rows, 8), rows)].astype(BF16)


def fold(blocks, plan_ref, pieces, folded):
    e = lax.axis_index("expert")
    folded[...] = jnp.zeros_like(folded)
    for i, d in enumerate(blocks):
        p = plan_ref[e ^ d]
        piece = pieces[0][i] if len(pieces) == 1 else pieces[i][...]
        folded[p] = folded[p] + piece.astype(F32)


def adam_update(folded, master, moment, second):
    new_moment = 0.9 * moment + 0.1 * folded
    new_second = 0.95 * second + 0.05 * folded * folded
    first_hat = new_moment / (1.0 - 0.9**10)
    second_hat = new_second / (1.0 - 0.95**10)
    new_master = master - 0.01 * (first_hat / (jnp.sqrt(second_hat) + 1e-08) + 0.1 * master)
    return new_master, new_moment, new_second


def rows_kernel(blocks, count, plan_ref, *refs):
    pieces, (master_ref, moment_ref, second_ref) = refs[:count], refs[count : count + 3]
    outs, folded = refs[count + 3 : -1], refs[-1]
    e = lax.axis_index("expert")
    fold(blocks, plan_ref, pieces, folded)
    for p in range(folded.shape[0]):
        folded[p] = adam_update(folded[p], master_ref[p], moment_ref[p], second_ref[p])[0]
    for i, d in enumerate(blocks):
        row = folded[plan_ref[e ^ d]].astype(BF16)
        if len(outs) == 1:
            outs[0][i] = row
        else:
            outs[i][...] = row


def state_kernel(blocks, count, plan_ref, *refs):
    pieces, (master_ref, moment_ref, second_ref) = refs[:count], refs[count : count + 3]
    new_master, new_moment, new_second, folded = refs[count + 3 :]
    fold(blocks, plan_ref, pieces, folded)
    for p in range(folded.shape[0]):
        new_master[p], new_moment[p], new_second[p] = adam_update(
            folded[p], master_ref[p], moment_ref[p], second_ref[p]
        )


def unpack_kernel(blocks, place_ref, *refs):
    parts, out_ref = refs[:-1], refs[-1]
    place = place_ref[...].T
    if len(parts) > 1:
        parts = [parts[blocks.index(d)] for d in range(len(parts))]
    for cols in columns(out_ref.shape[1]):
        rows = [p[:, cols] for p in parts]
        rows = rows[0] if len(rows) == 1 else jnp.concatenate(rows, axis=0)
        out_ref[:, cols] = dot(place, rows, NN).astype(BF16)


def order_kernel(blocks, *refs):
    e = lax.axis_index("expert")
    for i, d in enumerate(blocks):
        refs[-1][e ^ d] = refs[i][...]


def swap(x, axis, mask):
    size = lax.axis_size(axis)
    return lax.ppermute(x, axis, [(i, i ^ mask) for i in range(size)])


def order(n):
    return [0, n // 2, *(d for d in range(1, n) if d != n // 2)]


def exchange(blocks):
    return [
        swap(block, "expert", d) if d else block
        for d, block in zip(order(len(blocks)), blocks, strict=True)
    ]


def exchange_whole(x):
    flip = jnp.arange(x.shape[0], dtype=jnp.int32) ^ lax.axis_index("expert")
    x = jnp.take(x, flip, axis=0)
    x = lax.all_to_all(x, "expert", split_axis=0, concat_axis=0, tiled=True)
    return jnp.take(x, flip, axis=0)


def body(
    tokens, out_grad, routing, plan, gate_weight, up_weight, down_weight, master, moment, second
):
    n, m = lax.axis_size("expert"), lax.axis_size("slot")
    owned, width = tokens.shape
    capacity = 2 * owned // n
    part = down_weight.shape[1]
    owner = part // n
    rows = n * capacity
    few = capacity % 16 == 0
    ways = order(n) if few else list(range(n))
    shape = jax.ShapeDtypeStruct

    weights = [jnp.swapaxes(w, 1, 2)[0] for w in (gate_weight, up_weight)] + [down_weight[0]]
    outs = [shape((rows, owned), BF16), shape((3 * part, width), BF16)]
    outs += [shape((2 * capacity, width), BF16)] * n if few else [shape((rows, width), BF16)] * 2
    place, joined, *packed = call(
        functools.partial(pack_kernel, n, capacity, few),
        outs,
        (routing.reshape(1, owned), tokens, out_grad, *weights),
        scratch=[
            pltpu.VMEM((owned, width), BF16),
            pltpu.VMEM((owned, width), BF16),
            pltpu.SemaphoreType.DMA((5,)),
        ],
        far=range(1, 6),
        name="pack_rows",
        mib=56,
        flops=4 * owned * rows * width,
    )
    held = {0: joined}
    for mask in [1 << i for i in range(1, m.bit_length() - 1)][::-1]:
        for r in sorted(held):
            held[r | mask] = swap(held[r], "slot", mask)
    near = [joined, swap(joined, "slot", 1)]
    if few:
        blocks = exchange([packed[d] for d in ways])
    else:
        x, g = (
            exchange_whole(p.reshape(n, capacity, width)).reshape(rows, width) for p in packed
        )
        blocks = [jnp.concatenate((x, g), axis=0)]
    nb = len(blocks)
    blocks, held, near = lax.optimization_barrier((blocks, held, near))
    far = []
    for r in range(2, m, 2):
        far += [held[r], swap(held[r], "slot", 1)]
    nf = len(far)

    send, keep, partial = call(
        functools.partial(near_kernel, nb, 2),
        [shape((part, width), BF16), shape((part, width), BF16), shape((rows, width), F32)],
        (*blocks, *near),
        scratch=[pltpu.VMEM((2, part, rows), BF16), pltpu.VMEM((rows, 4 * part), BF16)],
        name="near_units",
        flops=24 * rows * width * part,
    )
    first = [keep, swap(send, "slot", 1)]
    far, partial = lax.optimization_barrier((far, partial))
    send, keep, a, b = call(
        functools.partial(hidden_kernel, nb, nf),
        [shape((nf // 2 * part, width), BF16)] * 2 + [shape((nf, part, rows), F32)] * 2,
        (*blocks, *far),
        scratch=[pltpu.VMEM((nf, part, rows), BF16)],
        name="far_units",
        flops=6 * rows * width * part * nf,
    )
    dx = call(
        functools.partial(back_kernel, nb, nf),
        [shape((r.shape[0] // 2, width), BF16) for r in blocks],
        (*blocks, *far, a, b, partial),
        scratch=[pltpu.VMEM((rows, nf * 2 * part), BF16)],
        name="input_gradient",
        flops=6 * rows * width * part * nf,
    )
    rest = call(
        add_kernel,
        [shape((part, width), BF16)] * (nf // 2),
        (keep, swap(send, "slot", 1)),
        name="add_pair",
    )
    rest = [swap(r, "slot", 2 * i) for i, r in enumerate(rest, 1)]
    if few:
        returned = exchange(dx)
        ahead = min(EARLY, n)
        returned[:ahead], rest = lax.optimization_barrier((returned[:ahead], rest))
    else:
        returned = [exchange_whole(dx[0].reshape(n, capacity, width)).reshape(rows, width)]
    pieces = call(
        functools.partial(cut_kernel, len(first) + len(rest), ways),
        [shape((owner, width), BF16)] * n if few else [shape((part, width), BF16)],
        (*first, *rest),
        scratch=[pltpu.VMEM((part, width), F32)],
        name="cut_gradient",
    )
    if few:
        arrived = exchange(pieces)
    else:
        flip = jnp.arange(n, dtype=jnp.int32) ^ lax.axis_index("expert")
        arrived = [exchange_whole(jnp.take(pieces[0].reshape(n, owner, width), flip, axis=0))]
    state = (plan, *arrived, master, moment, second)
    outgoing = call(
        functools.partial(rows_kernel, ways, len(arrived)),
        [shape((owner, width), BF16)] * n if few else [shape((n, owner, width), BF16)],
        state,
        scratch=[pltpu.VMEM(master.shape, F32)],
        smem=(0,),
        name="new_rows",
    )
    new_master, new_moment, new_second = call(
        functools.partial(state_kernel, ways, len(arrived)),
        [shape(master.shape, F32)] * 3,
        state,
        scratch=[pltpu.VMEM(master.shape, F32)],
        smem=(0,),
        name="new_state",
    )
    (token_grad,) = call(
        functools.partial(unpack_kernel, ways),
        [shape((owned, width), BF16)],
        (place, *returned),
        name="unpack_rows",
        flops=2 * owned * rows * width,
    )
    if few:
        (fresh,) = call(
            functools.partial(order_kernel, ways),
            [shape((n, owner, width), BF16)],
            exchange(outgoing),
            name="order_rows",
        )
    else:
        fresh = exchange_whole(outgoing[0])
    return (token_grad, new_master, new_moment, new_second, fresh.reshape(1, part, width))


def solution(mesh):
    rows, state = P(("expert", "slot"), None), P(None, ("slot", "expert"), None)
    split, held = P("expert", None, "slot"), P("expert", "slot", None)
    return jax.shard_map(
        body,
        mesh=mesh,
        in_specs=(rows, rows, rows, P(), split, split, held, state, state, state),
        out_specs=(rows, state, state, state, held),
        check_vma=False,
    )
```

```python
import functools

import jax
import jax.numpy as jnp
from jax import lax
from jax.experimental import pallas as pl
from jax.experimental.pallas import tpu as pltpu
from jax.sharding import PartitionSpec as P

BF16 = jnp.bfloat16
F32 = jnp.float32
NT = (((1,), (1,)), ((), ()))
TN = (((0,), (0,)), ((), ()))
NN = (((1,), (0,)), ((), ()))
COLUMNS = 512
EARLY = 4


def dot(a, b, dims):
    return lax.dot_general(a, b, dims, preferred_element_type=F32)


def call(kernel, outs, args, scratch=(), smem=(), far=(), name=None, mib=40, flops=0):
    moved = sum(a.size * a.dtype.itemsize for a in args) + sum(
        o.size * o.dtype.itemsize for o in outs
    )
    return pl.pallas_call(
        kernel,
        out_shape=tuple(outs),
        in_specs=[
            pl.BlockSpec(
                memory_space=pltpu.SMEM if i in smem else pl.ANY if i in far else pltpu.VMEM
            )
            for i in range(len(args))
        ],
        out_specs=tuple(pl.BlockSpec(memory_space=pltpu.VMEM) for _ in outs),
        scratch_shapes=list(scratch),
        compiler_params=pltpu.CompilerParams(vmem_limit_bytes=mib * 2**20),
        cost_estimate=pl.CostEstimate(flops=flops, bytes_accessed=moved, transcendentals=0),
        name=name,
    )(*args)


def columns(width):
    step = min(COLUMNS, width)
    return [slice(c, c + step) for c in range(0, width, step)]


def pack_kernel(n, capacity, joint, r_ref, x_ref, g_ref, place_ref, *outs):
    e = lax.axis_index("expert")
    owned, width = x_ref.shape
    rel = r_ref[...] ^ e
    block = lax.broadcasted_iota(jnp.int32, (n, owned), 0)
    match = (rel == block).astype(F32)
    upper = lax.broadcasted_iota(jnp.int32, (owned, owned), 0) <= lax.broadcasted_iota(
        jnp.int32, (owned, owned), 1
    )
    count = dot(match.astype(BF16), upper.astype(BF16), NN)
    pos = jnp.sum(match * (count - 1.0 + (block * capacity).astype(F32)), axis=0, keepdims=True)
    spot = lax.broadcasted_iota(jnp.int32, (n * capacity, owned), 0)
    place = (pos.astype(jnp.int32) == spot).astype(BF16)
    place_ref[...] = place
    for half, ref in enumerate((x_ref, g_ref)):
        for cols in columns(width):
            packed = dot(place, ref[:, cols], NN).astype(BF16)
            if joint:
                for d in range(n):
                    outs[d][half * capacity : (half + 1) * capacity, cols] = packed[
                        d * capacity : (d + 1) * capacity
                    ]
            else:
                outs[half][:, cols] = packed


def halves(blocks, half):
    parts = []
    for ref in blocks:
        rows = ref.shape[0] // 2
        parts.append(ref[half * rows : (half + 1) * rows])
    return parts[0] if len(parts) == 1 else jnp.concatenate(parts, axis=0)


def join_kernel(*refs):
    parts, out_ref, sem = refs[:-2], refs[-2], refs[-1]
    start, copies = 0, []
    for i, ref in enumerate(parts):
        rows = ref.shape[0]
        copies.append(pltpu.make_async_copy(ref, out_ref.at[start : start + rows], sem.at[i]))
        copies[i].start()
        start += rows
    for copy in copies:
        copy.wait()


def forward(weight, x):
    part = weight.shape[0] // 3
    both = dot(weight[: 2 * part], x, NT)
    gate, up = both[:part], both[part:]
    sig = jax.nn.sigmoid(gate)
    silu = gate * sig
    return (silu * up).astype(BF16), up * sig * (1.0 + gate * (1.0 - sig)), silu


def weight_gradient(hidden, g, send_ref, keep_ref):
    part = hidden.shape[1]
    for r in range(hidden.shape[0]):
        rows = slice(r // 2 * part, (r // 2 + 1) * part)
        for cols in columns(g.shape[1]):
            value = dot(hidden[r], g[:, cols], NN).astype(BF16)
            (send_ref if r % 2 else keep_ref)[rows, cols] = value


def turn(weight, g, a, b):
    part = weight.shape[0] // 3
    dh = dot(weight[2 * part :], g, NT)
    both = jnp.concatenate(((dh * a).astype(BF16), (dh * b).astype(BF16)), axis=0)
    return both.T


def input_gradient(turned, weights, cols):
    wide = weights[0].shape[0] // 3 * 2
    total = None
    for r, weight in enumerate(weights):
        term = dot(turned[:, r * wide : (r + 1) * wide], weight[:wide, cols], NN)
        total = term if total is None else total + term
    return total


def near_kernel(nb, nw, *refs):
    blocks, weights = refs[:nb], refs[nb : nb + nw]
    send_ref, keep_ref, partial_ref, hidden, turned = refs[nb + nw :]
    x, g = halves(blocks, 0), halves(blocks, 1)
    wide = weights[0].shape[0] // 3 * 2
    for r in range(nw):
        hidden[r], a, b = forward(weights[r], x)
        turned[:, r * wide : (r + 1) * wide] = turn(weights[r], g, a, b)
    weight_gradient(hidden, g, send_ref, keep_ref)
    for cols in columns(g.shape[1]):
        partial_ref[:, cols] = input_gradient(turned, weights, cols)


def hidden_kernel(nb, nw, *refs):
    blocks, weights = refs[:nb], refs[nb : nb + nw]
    send_ref, keep_ref, a_ref, b_ref, hidden = refs[nb + nw :]
    x, g = halves(blocks, 0), halves(blocks, 1)
    for r in range(nw):
        hidden[r], a_ref[r], b_ref[r] = forward(weights[r], x)
    weight_gradient(hidden, g, send_ref, keep_ref)


def back_kernel(nb, nw, *refs):
    blocks, weights = refs[:nb], refs[nb : nb + nw]
    a_ref, b_ref, partial_ref = refs[nb + nw : nb + nw + 3]
    outs, turned = refs[nb + nw + 3 : -1], refs[-1]
    g = halves(blocks, 1)
    wide = weights[0].shape[0] // 3 * 2
    for r in range(nw):
        turned[:, r * wide : (r + 1) * wide] = turn(weights[r], g, a_ref[r], b_ref[r])
    for cols in columns(g.shape[1]):
        total = (partial_ref[:, cols] + input_gradient(turned, weights, cols)).astype(BF16)
        start = 0
        for out in outs:
            out[:, cols] = total[start : start + out.shape[0]]
            start += out.shape[0]


def add_kernel(keep_ref, got_ref, *outs):
    part = outs[0].shape[0]
    for i, out in enumerate(outs):
        rows = slice(i * part, (i + 1) * part)
        out[...] = (keep_ref[rows].astype(F32) + got_ref[rows].astype(F32)).astype(BF16)


def cut_kernel(count, blocks, *refs):
    terms, outs, sums = refs[:count], refs[count:-1], refs[-1]
    e = lax.axis_index("expert")
    total = terms[0][...].astype(F32)
    for ref in terms[1:]:
        total = total + ref[...].astype(F32)
    if len(outs) == 1:
        outs[0][...] = total.astype(BF16)
        return
    sums[...] = total
    rows = outs[0].shape[0]
    for d, out in zip(blocks, outs, strict=True):
        out[...] = sums[pl.ds(pl.multiple_of((e ^ d) * rows, 8), rows)].astype(BF16)


def fold(blocks, plan_ref, pieces, folded):
    e = lax.axis_index("expert")
    folded[...] = jnp.zeros_like(folded)
    for i, d in enumerate(blocks):
        p = plan_ref[e ^ d]
        piece = pieces[0][i] if len(pieces) == 1 else pieces[i][...]
        folded[p] = folded[p] + piece.astype(F32)


def adam_update(folded, master, moment, second):
    new_moment = 0.9 * moment + 0.1 * folded
    new_second = 0.95 * second + 0.05 * folded * folded
    first_hat = new_moment / (1.0 - 0.9**10)
    second_hat = new_second / (1.0 - 0.95**10)
    new_master = master - 0.01 * (first_hat / (jnp.sqrt(second_hat) + 1e-08) + 0.1 * master)
    return new_master, new_moment, new_second


def rows_kernel(blocks, count, plan_ref, *refs):
    pieces, (master_ref, moment_ref, second_ref) = refs[:count], refs[count : count + 3]
    outs, folded = refs[count + 3 : -1], refs[-1]
    e = lax.axis_index("expert")
    fold(blocks, plan_ref, pieces, folded)
    for p in range(folded.shape[0]):
        folded[p] = adam_update(folded[p], master_ref[p], moment_ref[p], second_ref[p])[0]
    for i, d in enumerate(blocks):
        row = folded[plan_ref[e ^ d]].astype(BF16)
        if len(outs) == 1:
            outs[0][i] = row
        else:
            outs[i][...] = row


def state_kernel(blocks, count, plan_ref, *refs):
    pieces, (master_ref, moment_ref, second_ref) = refs[:count], refs[count : count + 3]
    new_master, new_moment, new_second, folded = refs[count + 3 :]
    fold(blocks, plan_ref, pieces, folded)
    for p in range(folded.shape[0]):
        new_master[p], new_moment[p], new_second[p] = adam_update(
            folded[p], master_ref[p], moment_ref[p], second_ref[p]
        )


def unpack_kernel(blocks, place_ref, *refs):
    parts, out_ref = refs[:-1], refs[-1]
    place = place_ref[...].T
    if len(parts) > 1:
        parts = [parts[blocks.index(d)] for d in range(len(parts))]
    for cols in columns(out_ref.shape[1]):
        rows = [p[:, cols] for p in parts]
        rows = rows[0] if len(rows) == 1 else jnp.concatenate(rows, axis=0)
        out_ref[:, cols] = dot(place, rows, NN).astype(BF16)


def order_kernel(blocks, *refs):
    e = lax.axis_index("expert")
    for i, d in enumerate(blocks):
        refs[-1][e ^ d] = refs[i][...]


def swap(x, axis, mask):
    size = lax.axis_size(axis)
    return lax.ppermute(x, axis, [(i, i ^ mask) for i in range(size)])


def order(n):
    return [0, n // 2, *(d for d in range(1, n) if d != n // 2)]


def crossing(n):
    long, short = list(range(n // 2, n)), list(range(1, n // 2))
    return [0, *long[: EARLY - 1], *short[:1], *long[EARLY - 1 :], *short[1:]]


def exchange(blocks, ways):
    return [swap(blocks[d], "expert", d) if d else blocks[d] for d in ways]


def exchange_whole(x):
    flip = jnp.arange(x.shape[0], dtype=jnp.int32) ^ lax.axis_index("expert")
    x = jnp.take(x, flip, axis=0)
    x = lax.all_to_all(x, "expert", split_axis=0, concat_axis=0, tiled=True)
    return jnp.take(x, flip, axis=0)


def body(
    tokens, out_grad, routing, plan, gate_weight, up_weight, down_weight, master, moment, second
):
    n, m = lax.axis_size("expert"), lax.axis_size("slot")
    owned, width = tokens.shape
    capacity = 2 * owned // n
    part = down_weight.shape[1]
    owner = part // n
    rows = n * capacity
    few = capacity % 16 == 0
    ways = order(n) if few else list(range(n))
    shape = jax.ShapeDtypeStruct

    weights = [jnp.swapaxes(w, 1, 2)[0] for w in (gate_weight, up_weight)] + [down_weight[0]]
    (joined,) = call(
        join_kernel,
        [shape((3 * part, width), BF16)],
        weights,
        scratch=[pltpu.SemaphoreType.DMA((3,))],
        far=range(3),
        name="join_weights",
        mib=16,
    )
    outs = [shape((rows, owned), BF16)]
    outs += [shape((2 * capacity, width), BF16)] * n if few else [shape((rows, width), BF16)] * 2
    place, *packed = call(
        functools.partial(pack_kernel, n, capacity, few),
        outs,
        (routing.reshape(1, owned), tokens, out_grad),
        name="pack_rows",
        flops=4 * owned * rows * width,
    )
    if few:
        blocks = exchange(packed, ways)
    else:
        x, g = (
            exchange_whole(p.reshape(n, capacity, width)).reshape(rows, width) for p in packed
        )
        blocks = [jnp.concatenate((x, g), axis=0)]
    nb = len(blocks)

    held = {0: joined}
    for mask in [1 << i for i in range(1, m.bit_length() - 1)][::-1]:
        for r in sorted(held):
            held[r | mask] = swap(held[r], "slot", mask)
    middle = nb // 2
    neighbour, blocks[middle] = lax.optimization_barrier((joined, blocks[middle]))
    near = [joined, swap(neighbour, "slot", 1)]
    came, held = lax.optimization_barrier((blocks[1:], [held[r] for r in range(2, m, 2)]))
    blocks[1:] = came
    far = [w for v in held for w in (v, swap(v, "slot", 1))]
    nf = len(far)

    send, kept, partial = call(
        functools.partial(near_kernel, nb, 2),
        [shape((part, width), BF16), shape((part, width), BF16), shape((rows, width), F32)],
        (*blocks, *near),
        scratch=[pltpu.VMEM((2, part, rows), BF16), pltpu.VMEM((rows, 4 * part), BF16)],
        name="near_units",
        flops=24 * rows * width * part,
    )
    first = [kept, swap(send, "slot", 1)]
    far, partial = lax.optimization_barrier((far, partial))
    send, keep, a, b = call(
        functools.partial(hidden_kernel, nb, nf),
        [shape((nf // 2 * part, width), BF16)] * 2 + [shape((nf, part, rows), F32)] * 2,
        (*blocks, *far),
        scratch=[pltpu.VMEM((nf, part, rows), BF16)],
        name="far_units",
        flops=6 * rows * width * part * nf,
    )
    got = swap(send, "slot", 1)
    dx = call(
        functools.partial(back_kernel, nb, nf),
        [shape((r.shape[0] // 2, width), BF16) for r in blocks],
        (*blocks, *far, a, b, partial),
        scratch=[pltpu.VMEM((rows, nf * 2 * part), BF16)],
        name="input_gradient",
        flops=6 * rows * width * part * nf,
    )
    got, dx = lax.optimization_barrier((got, dx))
    rest = call(
        add_kernel,
        [shape((part, width), BF16)] * (nf // 2),
        (keep, got),
        name="add_pair",
    )
    rest = [swap(r, "slot", 2 * i) for i, r in enumerate(rest, 1)]
    back = crossing(n) if few else ways
    if few:
        returned = exchange(dict(zip(ways, dx, strict=True)), back)
        returned[1:EARLY], rest = lax.optimization_barrier((returned[1:EARLY], rest))
    else:
        returned = [exchange_whole(dx[0].reshape(n, capacity, width)).reshape(rows, width)]
    pieces = call(
        functools.partial(cut_kernel, len(first) + len(rest), ways),
        [shape((owner, width), BF16)] * n if few else [shape((part, width), BF16)],
        (*first, *rest),
        scratch=[pltpu.VMEM((part, width), F32)],
        name="cut_gradient",
    )
    if few:
        arrived = exchange(dict(zip(ways, pieces, strict=True)), ways)
    else:
        flip = jnp.arange(n, dtype=jnp.int32) ^ lax.axis_index("expert")
        arrived = [exchange_whole(jnp.take(pieces[0].reshape(n, owner, width), flip, axis=0))]
    state = (plan, *arrived, master, moment, second)
    outgoing = call(
        functools.partial(rows_kernel, ways, len(arrived)),
        [shape((owner, width), BF16)] * n if few else [shape((n, owner, width), BF16)],
        state,
        scratch=[pltpu.VMEM(master.shape, F32)],
        smem=(0,),
        name="new_rows",
    )
    new_master, new_moment, new_second = call(
        functools.partial(state_kernel, ways, len(arrived)),
        [shape(master.shape, F32)] * 3,
        state,
        scratch=[pltpu.VMEM(master.shape, F32)],
        smem=(0,),
        name="new_state",
    )
    (token_grad,) = call(
        functools.partial(unpack_kernel, back),
        [shape((owned, width), BF16)],
        (place, *returned),
        name="unpack_rows",
        flops=2 * owned * rows * width,
    )
    if few:
        (fresh,) = call(
            functools.partial(order_kernel, ways),
            [shape((n, owner, width), BF16)],
            exchange(dict(zip(ways, outgoing, strict=True)), ways),
            name="order_rows",
        )
    else:
        fresh = exchange_whole(outgoing[0])
    return (token_grad, new_master, new_moment, new_second, fresh.reshape(1, part, width))


def solution(mesh):
    rows, state = P(("expert", "slot"), None), P(None, ("slot", "expert"), None)
    split, held = P("expert", None, "slot"), P("expert", "slot", None)
    return jax.shard_map(
        body,
        mesh=mesh,
        in_specs=(rows, rows, rows, P(), split, split, held, state, state, state),
        out_specs=(rows, state, state, state, held),
        check_vma=False,
    )
```

```python
import functools

import jax
import jax.numpy as jnp
from jax import lax
from jax.experimental import pallas as pl
from jax.experimental.pallas import tpu as pltpu
from jax.sharding import PartitionSpec as P

BF16 = jnp.bfloat16
F32 = jnp.float32
NT = (((1,), (1,)), ((), ()))
TN = (((0,), (0,)), ((), ()))
NN = (((1,), (0,)), ((), ()))
COLUMNS = 512
PIECES = 6
OUT = 3
NEWFLOPS = 2 * 10**9


def dot(a, b, dims):
    return lax.dot_general(a, b, dims, preferred_element_type=F32)


def call(kernel, outs, args, scratch=(), smem=(), far=(), name=None, mib=40, flops=0):
    moved = sum(a.size * a.dtype.itemsize for a in args) + sum(
        o.size * o.dtype.itemsize for o in outs
    )
    return pl.pallas_call(
        kernel,
        out_shape=tuple(outs),
        in_specs=[
            pl.BlockSpec(
                memory_space=pltpu.SMEM if i in smem else pl.ANY if i in far else pltpu.VMEM
            )
            for i in range(len(args))
        ],
        out_specs=tuple(pl.BlockSpec(memory_space=pltpu.VMEM) for _ in outs),
        scratch_shapes=list(scratch),
        compiler_params=pltpu.CompilerParams(vmem_limit_bytes=mib * 2**20),
        cost_estimate=pl.CostEstimate(flops=flops, bytes_accessed=moved, transcendentals=0),
        name=name,
    )(*args)


def columns(width):
    step = min(COLUMNS, width)
    return [slice(c, c + step) for c in range(0, width, step)]


def pack_kernel(n, capacity, joint, r_ref, x_ref, g_ref, place_ref, *outs):
    e = lax.axis_index("expert")
    owned, width = x_ref.shape
    rel = r_ref[...] ^ e
    block = lax.broadcasted_iota(jnp.int32, (n, owned), 0)
    match = (rel == block).astype(F32)
    upper = lax.broadcasted_iota(jnp.int32, (owned, owned), 0) <= lax.broadcasted_iota(
        jnp.int32, (owned, owned), 1
    )
    count = dot(match.astype(BF16), upper.astype(BF16), NN)
    pos = jnp.sum(match * (count - 1.0 + (block * capacity).astype(F32)), axis=0, keepdims=True)
    spot = lax.broadcasted_iota(jnp.int32, (n * capacity, owned), 0)
    place = (pos.astype(jnp.int32) == spot).astype(BF16)
    place_ref[...] = place
    for half, ref in enumerate((x_ref, g_ref)):
        for cols in columns(width):
            packed = dot(place, ref[:, cols], NN).astype(BF16)
            if joint:
                for d in range(n):
                    outs[d][half * capacity : (half + 1) * capacity, cols] = packed[
                        d * capacity : (d + 1) * capacity
                    ]
            else:
                outs[half][:, cols] = packed


def halves(blocks, half):
    parts = []
    for ref in blocks:
        rows = ref.shape[0] // 2
        parts.append(ref[half * rows : (half + 1) * rows])
    return parts[0] if len(parts) == 1 else jnp.concatenate(parts, axis=0)


def forward(weight, x):
    part = weight.shape[0] // 3
    both = dot(weight[: 2 * part], x, NT)
    gate, up = both[:part], both[part:]
    sig = jax.nn.sigmoid(gate)
    silu = gate * sig
    return (silu * up).astype(BF16), up * sig * (1.0 + gate * (1.0 - sig)), silu


def weight_gradient(hidden, g, send_ref, keep_ref):
    part = hidden.shape[1]
    for r in range(hidden.shape[0]):
        rows = slice(r // 2 * part, (r // 2 + 1) * part)
        for cols in columns(g.shape[1]):
            value = dot(hidden[r], g[:, cols], NN).astype(BF16)
            (send_ref if r % 2 else keep_ref)[rows, cols] = value


def turn(weight, g, a, b):
    part = weight.shape[0] // 3
    dh = dot(weight[2 * part :], g, NT)
    both = jnp.concatenate(((dh * a).astype(BF16), (dh * b).astype(BF16)), axis=0)
    return both.T


def input_gradient(turned, weights, cols):
    wide = weights[0].shape[0] // 3 * 2
    total = None
    for r, weight in enumerate(weights):
        term = dot(turned[:, r * wide : (r + 1) * wide], weight[:wide, cols], NN)
        total = term if total is None else total + term
    return total


def near_kernel(nb, nw, *refs):
    blocks, weights = refs[:nb], refs[nb : nb + nw]
    send_ref, keep_ref, partial_ref, hidden, turned = refs[nb + nw :]
    x, g = halves(blocks, 0), halves(blocks, 1)
    wide = weights[0].shape[0] // 3 * 2
    for r in range(nw):
        hidden[r], a, b = forward(weights[r], x)
        turned[:, r * wide : (r + 1) * wide] = turn(weights[r], g, a, b)
    weight_gradient(hidden, g, send_ref, keep_ref)
    for cols in columns(g.shape[1]):
        partial_ref[:, cols] = input_gradient(turned, weights, cols)


def hidden_kernel(nb, nw, *refs):
    blocks, weights = refs[:nb], refs[nb : nb + nw]
    send_ref, keep_ref, a_ref, b_ref, hidden = refs[nb + nw :]
    x, g = halves(blocks, 0), halves(blocks, 1)
    for r in range(nw):
        hidden[r], a_ref[r], b_ref[r] = forward(weights[r], x)
    weight_gradient(hidden, g, send_ref, keep_ref)


def back_kernel(nb, nw, *refs):
    blocks, weights = refs[:nb], refs[nb : nb + nw]
    a_ref, b_ref, partial_ref = refs[nb + nw : nb + nw + 3]
    outs, turned = refs[nb + nw + 3 : -1], refs[-1]
    g = halves(blocks, 1)
    wide = weights[0].shape[0] // 3 * 2
    for r in range(nw):
        turned[:, r * wide : (r + 1) * wide] = turn(weights[r], g, a_ref[r], b_ref[r])
    for cols in columns(g.shape[1]):
        total = (partial_ref[:, cols] + input_gradient(turned, weights, cols)).astype(BF16)
        start = 0
        for out in outs:
            out[:, cols] = total[start : start + out.shape[0]]
            start += out.shape[0]


def add_kernel(keep_ref, got_ref, *outs):
    part = outs[0].shape[0]
    for i, out in enumerate(outs):
        rows = slice(i * part, (i + 1) * part)
        out[...] = (keep_ref[rows].astype(F32) + got_ref[rows].astype(F32)).astype(BF16)


def cut_kernel(count, blocks, *refs):
    terms, outs, sums = refs[:count], refs[count:-1], refs[-1]
    e = lax.axis_index("expert")
    total = terms[0][...].astype(F32)
    for ref in terms[1:]:
        total = total + ref[...].astype(F32)
    if len(outs) == 1:
        outs[0][...] = total.astype(BF16)
        return
    sums[...] = total
    rows = outs[0].shape[0]
    for d, out in zip(blocks, outs, strict=True):
        out[...] = sums[pl.ds(pl.multiple_of((e ^ d) * rows, 8), rows)].astype(BF16)


def fold(blocks, plan_ref, pieces, folded):
    e = lax.axis_index("expert")
    folded[...] = jnp.zeros_like(folded)
    for i, d in enumerate(blocks):
        p = plan_ref[e ^ d]
        piece = pieces[0][i] if len(pieces) == 1 else pieces[i][...]
        folded[p] = folded[p] + piece.astype(F32)


def adam_update(folded, master, moment, second):
    new_moment = 0.9 * moment + 0.1 * folded
    new_second = 0.95 * second + 0.05 * folded * folded
    first_hat = new_moment * (1.0 / (1.0 - 0.9**10))
    second_hat = new_second * (1.0 / (1.0 - 0.95**10))
    new_master = master - 0.01 * (first_hat / (jnp.sqrt(second_hat) + 1e-08) + 0.1 * master)
    return new_master, new_moment, new_second


def rows_kernel(blocks, new, count, plan_ref, *refs):
    pieces, (master_ref, moment_ref, second_ref) = refs[:count], refs[count : count + 3]
    outs, folded = refs[count + 3 : -1], refs[-1]
    e = lax.axis_index("expert")
    fold(blocks, plan_ref, pieces, folded)
    for p in range(folded.shape[0]):
        folded[p] = adam_update(folded[p], master_ref[p], moment_ref[p], second_ref[p])[0]
    for i, d in enumerate(new):
        row = folded[plan_ref[e ^ d]].astype(BF16)
        if len(outs) == 1:
            outs[0][i] = row
        else:
            outs[i][...] = row


def state_kernel(blocks, count, plan_ref, *refs):
    pieces, (master_ref, moment_ref, second_ref) = refs[:count], refs[count : count + 3]
    new_master, new_moment, new_second, folded = refs[count + 3 :]
    fold(blocks, plan_ref, pieces, folded)
    for p in range(folded.shape[0]):
        new_master[p], new_moment[p], new_second[p] = adam_update(
            folded[p], master_ref[p], moment_ref[p], second_ref[p]
        )


def unpack_kernel(blocks, place_ref, *refs):
    parts, out_ref = refs[:-1], refs[-1]
    place = place_ref[...].T
    if len(parts) > 1:
        parts = [parts[blocks.index(d)] for d in range(len(parts))]
    for cols in columns(out_ref.shape[1]):
        rows = [p[:, cols] for p in parts]
        rows = rows[0] if len(rows) == 1 else jnp.concatenate(rows, axis=0)
        out_ref[:, cols] = dot(place, rows, NN).astype(BF16)


def order_kernel(blocks, *refs):
    e = lax.axis_index("expert")
    for i, d in enumerate(blocks):
        refs[-1][e ^ d] = refs[i][...]


def swap(x, axis, mask):
    size = lax.axis_size(axis)
    return lax.ppermute(x, axis, [(i, i ^ mask) for i in range(size)])


def order(n):
    return [0, n // 2, *(d for d in range(1, n) if d != n // 2)]


def crossing(n):
    return [0, *range(n // 2, n - 1), *range(1, n // 2), n - 1]


def by_turns(n):
    return [0, *(d for r in range(n // 2) for d in (n // 2 + r, r + 1))][:n]


def exchange(blocks, ways):
    return [swap(blocks[d], "expert", d) if d else blocks[d] for d in ways]


def exchange_whole(x):
    flip = jnp.arange(x.shape[0], dtype=jnp.int32) ^ lax.axis_index("expert")
    x = jnp.take(x, flip, axis=0)
    x = lax.all_to_all(x, "expert", split_axis=0, concat_axis=0, tiled=True)
    return jnp.take(x, flip, axis=0)


def after(*values):
    return lax.optimization_barrier(values)


def body(
    tokens, out_grad, routing, plan, gate_weight, up_weight, down_weight, master, moment, second
):
    n, m = lax.axis_size("expert"), lax.axis_size("slot")
    owned, width = tokens.shape
    capacity = 2 * owned // n
    part = down_weight.shape[1]
    owner = part // n
    rows = n * capacity
    few = capacity % 16 == 0
    ways = order(n) if few else list(range(n))
    mixed = by_turns(n) if few else ways
    shape = jax.ShapeDtypeStruct

    weights = [jnp.swapaxes(w, 1, 2)[0] for w in (gate_weight, up_weight)] + [down_weight[0]]
    joined = jnp.concatenate(weights, axis=0)
    outs = [shape((rows, owned), BF16)]
    outs += [shape((2 * capacity, width), BF16)] * n if few else [shape((rows, width), BF16)] * 2
    place, *packed = call(
        functools.partial(pack_kernel, n, capacity, few),
        outs,
        (routing.reshape(1, owned), tokens, out_grad),
        name="pack_rows",
        flops=4 * owned * rows * width,
    )
    if few:
        blocks = exchange(packed, mixed)
    else:
        x, g = (
            exchange_whole(p.reshape(n, capacity, width)).reshape(rows, width) for p in packed
        )
        blocks = [jnp.concatenate((x, g), axis=0)]
    nb = len(blocks)

    held = {0: joined}
    for mask in [1 << i for i in range(1, m.bit_length() - 1)][::-1]:
        for r in sorted(held):
            held[r | mask] = swap(held[r], "slot", mask)
    middle = nb // 2
    neighbour, blocks[middle] = lax.optimization_barrier((joined, blocks[middle]))
    near = [joined, swap(neighbour, "slot", 1)]
    came, held = lax.optimization_barrier((blocks[1:], [held[r] for r in range(2, m, 2)]))
    blocks[1:] = came
    far = [w for v in held for w in (v, swap(v, "slot", 1))]
    nf = len(far)

    send, kept, partial = call(
        functools.partial(near_kernel, nb, 2),
        [shape((part, width), BF16), shape((part, width), BF16), shape((rows, width), F32)],
        (*blocks, *near),
        scratch=[pltpu.VMEM((2, part, rows), BF16), pltpu.VMEM((rows, 4 * part), BF16)],
        name="near_units",
        flops=24 * rows * width * part,
    )
    first = [kept, swap(send, "slot", 1)]
    far, partial = lax.optimization_barrier((far, partial))
    send, keep, a, b = call(
        functools.partial(hidden_kernel, nb, nf),
        [shape((nf // 2 * part, width), BF16)] * 2 + [shape((nf, part, rows), F32)] * 2,
        (*blocks, *far),
        scratch=[pltpu.VMEM((nf, part, rows), BF16)],
        name="far_units",
        flops=6 * rows * width * part * nf,
    )
    got = swap(send, "slot", 1)
    dx = call(
        functools.partial(back_kernel, nb, nf),
        [shape((r.shape[0] // 2, width), BF16) for r in blocks],
        (*blocks, *far, a, b, partial),
        scratch=[pltpu.VMEM((rows, nf * 2 * part), BF16)],
        name="input_gradient",
        flops=6 * rows * width * part * nf,
    )
    got, dx = after(got, list(dx))
    rest = call(
        add_kernel,
        [shape((part, width), BF16)] * (nf // 2),
        (keep, got),
        name="add_pair",
    )
    rest = [swap(r, "slot", 2 * i) for i, r in enumerate(rest, 1)]
    owner = part // n
    if few:
        back = crossing(n)
        dx = dict(zip(mixed, dx, strict=True))
        returned = exchange(dx, back[:-1])
        ahead = n // 2
        returned[1:ahead], rest = after(returned[1:ahead], rest)
    pieces = call(
        functools.partial(cut_kernel, len(first) + len(rest), ways),
        [shape((owner, width), BF16)] * n if few else [shape((part, width), BF16)],
        (*first, *rest),
        scratch=[pltpu.VMEM((part, width), F32)],
        name="cut_gradient",
    )
    if few:
        arrived = exchange(dict(zip(ways, pieces, strict=True)), ways)
        if PIECES:
            dx[n - 1], arrived[PIECES] = after(dx[n - 1], arrived[PIECES])
        returned += exchange(dx, back[-1:])
    else:
        back = ways
        returned = [exchange_whole(dx[0].reshape(n, capacity, width)).reshape(rows, width)]
        flip = jnp.arange(n, dtype=jnp.int32) ^ lax.axis_index("expert")
        arrived = [exchange_whole(jnp.take(pieces[0].reshape(n, owner, width), flip, axis=0))]
    state = (plan, *arrived, master, moment, second)
    outgoing = call(
        functools.partial(rows_kernel, ways, mixed, len(arrived)),
        [shape((owner, width), BF16)] * n if few else [shape((n, owner, width), BF16)],
        state,
        scratch=[pltpu.VMEM(master.shape, F32)],
        smem=(0,),
        name="new_rows",
        flops=NEWFLOPS,
    )
    if few and OUT:
        outgoing = list(outgoing)
        returned[-1], outgoing[OUT:] = after(returned[-1], outgoing[OUT:])
    new_master, new_moment, new_second = call(
        functools.partial(state_kernel, ways, len(arrived)),
        [shape(master.shape, F32)] * 3,
        state,
        scratch=[pltpu.VMEM(master.shape, F32)],
        smem=(0,),
        name="new_state",
    )
    (token_grad,) = call(
        functools.partial(unpack_kernel, back),
        [shape((owned, width), BF16)],
        (place, *returned),
        name="unpack_rows",
        flops=2 * owned * rows * width,
    )
    if few:
        (fresh,) = call(
            functools.partial(order_kernel, mixed),
            [shape((n, owner, width), BF16)],
            exchange(dict(zip(mixed, outgoing, strict=True)), mixed),
            name="order_rows",
        )
    else:
        fresh = exchange_whole(outgoing[0])
    return (token_grad, new_master, new_moment, new_second, fresh.reshape(1, part, width))


def solution(mesh):
    rows, state = P(("expert", "slot"), None), P(None, ("slot", "expert"), None)
    split, held = P("expert", None, "slot"), P("expert", "slot", None)
    return jax.shard_map(
        body,
        mesh=mesh,
        in_specs=(rows, rows, rows, P(), split, split, held, state, state, state),
        out_specs=(rows, state, state, state, held),
        check_vma=False,
    )
```

```python
import functools

import jax
import jax.numpy as jnp
from jax import lax
from jax.experimental import pallas as pl
from jax.experimental.pallas import tpu as pltpu
from jax.sharding import PartitionSpec as P

BF16 = jnp.bfloat16
F32 = jnp.float32
NT = (((1,), (1,)), ((), ()))
TN = (((0,), (0,)), ((), ()))
NN = (((1,), (0,)), ((), ()))
COLUMNS = 512
PIECES = 6
OUT = 3
NEWFLOPS = 2 * 10**9


def dot(a, b, dims):
    return lax.dot_general(a, b, dims, preferred_element_type=F32)


def call(kernel, outs, args, scratch=(), smem=(), far=(), name=None, mib=40, flops=0):
    moved = sum(a.size * a.dtype.itemsize for a in args) + sum(
        o.size * o.dtype.itemsize for o in outs
    )
    return pl.pallas_call(
        kernel,
        out_shape=tuple(outs),
        in_specs=[
            pl.BlockSpec(
                memory_space=pltpu.SMEM if i in smem else pl.ANY if i in far else pltpu.VMEM
            )
            for i in range(len(args))
        ],
        out_specs=tuple(pl.BlockSpec(memory_space=pltpu.VMEM) for _ in outs),
        scratch_shapes=list(scratch),
        compiler_params=pltpu.CompilerParams(vmem_limit_bytes=mib * 2**20),
        cost_estimate=pl.CostEstimate(flops=flops, bytes_accessed=moved, transcendentals=0),
        name=name,
    )(*args)


def columns(width):
    step = min(COLUMNS, width)
    return [slice(c, c + step) for c in range(0, width, step)]


def pack_kernel(n, capacity, joint, r_ref, x_ref, g_ref, place_ref, *outs):
    e = lax.axis_index("expert")
    owned, width = x_ref.shape
    rel = r_ref[...] ^ e
    block = lax.broadcasted_iota(jnp.int32, (n, owned), 0)
    match = (rel == block).astype(F32)
    upper = lax.broadcasted_iota(jnp.int32, (owned, owned), 0) <= lax.broadcasted_iota(
        jnp.int32, (owned, owned), 1
    )
    count = dot(match.astype(BF16), upper.astype(BF16), NN)
    pos = jnp.sum(match * (count - 1.0 + (block * capacity).astype(F32)), axis=0, keepdims=True)
    spot = lax.broadcasted_iota(jnp.int32, (n * capacity, owned), 0)
    place = (pos.astype(jnp.int32) == spot).astype(BF16)
    place_ref[...] = place
    for half, ref in enumerate((x_ref, g_ref)):
        for cols in columns(width):
            packed = dot(place, ref[:, cols], NN).astype(BF16)
            if joint:
                for d in range(n):
                    outs[d][half * capacity : (half + 1) * capacity, cols] = packed[
                        d * capacity : (d + 1) * capacity
                    ]
            else:
                outs[half][:, cols] = packed


def halves(blocks, half):
    parts = []
    for ref in blocks:
        rows = ref.shape[0] // 2
        parts.append(ref[half * rows : (half + 1) * rows])
    return parts[0] if len(parts) == 1 else jnp.concatenate(parts, axis=0)


def parted(weights, count):
    if len(weights) == 2 * count:
        return weights[:count], weights[count:]
    part = weights[0].shape[0] // 3
    return [w.at[: 2 * part] for w in weights], [w.at[2 * part :] for w in weights]


def forward(high, x):
    both = dot(high[...], x, NT)
    part = both.shape[0] // 2
    gate, up = both[:part], both[part:]
    sig = jax.nn.sigmoid(gate)
    silu = gate * sig
    return (silu * up).astype(BF16), up * sig * (1.0 + gate * (1.0 - sig)), silu


def weight_gradient(hidden, g, send_ref, keep_ref):
    part = hidden.shape[1]
    for r in range(hidden.shape[0]):
        rows = slice(r // 2 * part, (r // 2 + 1) * part)
        for cols in columns(g.shape[1]):
            value = dot(hidden[r], g[:, cols], NN).astype(BF16)
            (send_ref if r % 2 else keep_ref)[rows, cols] = value


def turn(low, g, a, b):
    dh = dot(low[...], g, NT)
    both = jnp.concatenate(((dh * a).astype(BF16), (dh * b).astype(BF16)), axis=0)
    return both.T


def input_gradient(turned, highs, cols):
    wide = highs[0].shape[0]
    total = None
    for r, high in enumerate(highs):
        term = dot(turned[:, r * wide : (r + 1) * wide], high[:, cols], NN)
        total = term if total is None else total + term
    return total


def near_kernel(nb, nw, *refs):
    blocks, weights = refs[:nb], refs[nb : nb + nw]
    send_ref, keep_ref, partial_ref, hidden, turned = refs[nb + nw :]
    x, g = halves(blocks, 0), halves(blocks, 1)
    highs, lows = parted(weights, nw)
    wide = highs[0].shape[0]
    for r in range(nw):
        hidden[r], a, b = forward(highs[r], x)
        turned[:, r * wide : (r + 1) * wide] = turn(lows[r], g, a, b)
    weight_gradient(hidden, g, send_ref, keep_ref)
    for cols in columns(g.shape[1]):
        partial_ref[:, cols] = input_gradient(turned, highs, cols)


def hidden_kernel(nb, nw, *refs):
    blocks, highs = refs[:nb], refs[nb : nb + nw]
    send_ref, keep_ref, a_ref, b_ref, hidden = refs[nb + nw :]
    x, g = halves(blocks, 0), halves(blocks, 1)
    for r in range(nw):
        hidden[r], a_ref[r], b_ref[r] = forward(highs[r], x)
    weight_gradient(hidden, g, send_ref, keep_ref)


def back_kernel(nb, nw, *refs):
    blocks, (highs, lows) = refs[:nb], parted(refs[nb : nb + 2 * nw], nw)
    a_ref, b_ref, partial_ref = refs[nb + 2 * nw : nb + 2 * nw + 3]
    outs, turned = refs[nb + 2 * nw + 3 : -1], refs[-1]
    g = halves(blocks, 1)
    wide = highs[0].shape[0]
    for r in range(nw):
        turned[:, r * wide : (r + 1) * wide] = turn(lows[r], g, a_ref[r], b_ref[r])
    for cols in columns(g.shape[1]):
        total = (partial_ref[:, cols] + input_gradient(turned, highs, cols)).astype(BF16)
        start = 0
        for out in outs:
            out[:, cols] = total[start : start + out.shape[0]]
            start += out.shape[0]


def add_kernel(keep_ref, got_ref, *outs):
    part = outs[0].shape[0]
    for i, out in enumerate(outs):
        rows = slice(i * part, (i + 1) * part)
        out[...] = (keep_ref[rows].astype(F32) + got_ref[rows].astype(F32)).astype(BF16)


def cut_kernel(count, blocks, *refs):
    terms, outs, sums = refs[:count], refs[count:-1], refs[-1]
    e = lax.axis_index("expert")
    total = terms[0][...].astype(F32)
    for ref in terms[1:]:
        total = total + ref[...].astype(F32)
    if len(outs) == 1:
        outs[0][...] = total.astype(BF16)
        return
    sums[...] = total
    rows = outs[0].shape[0]
    for d, out in zip(blocks, outs, strict=True):
        out[...] = sums[pl.ds(pl.multiple_of((e ^ d) * rows, 8), rows)].astype(BF16)


def fold(blocks, plan_ref, pieces, folded):
    e = lax.axis_index("expert")
    folded[...] = jnp.zeros_like(folded)
    for i, d in enumerate(blocks):
        p = plan_ref[e ^ d]
        piece = pieces[0][i] if len(pieces) == 1 else pieces[i][...]
        folded[p] = folded[p] + piece.astype(F32)


def adam_update(folded, master, moment, second):
    new_moment = 0.9 * moment + 0.1 * folded
    new_second = 0.95 * second + 0.05 * folded * folded
    first_hat = new_moment * (1.0 / (1.0 - 0.9**10))
    second_hat = new_second * (1.0 / (1.0 - 0.95**10))
    new_master = master - 0.01 * (first_hat / (jnp.sqrt(second_hat) + 1e-08) + 0.1 * master)
    return new_master, new_moment, new_second


def rows_kernel(blocks, new, count, plan_ref, *refs):
    pieces, (master_ref, moment_ref, second_ref) = refs[:count], refs[count : count + 3]
    outs, folded = refs[count + 3 : -1], refs[-1]
    e = lax.axis_index("expert")
    fold(blocks, plan_ref, pieces, folded)
    for p in range(folded.shape[0]):
        folded[p] = adam_update(folded[p], master_ref[p], moment_ref[p], second_ref[p])[0]
    for i, d in enumerate(new):
        row = folded[plan_ref[e ^ d]].astype(BF16)
        if len(outs) == 1:
            outs[0][i] = row
        else:
            outs[i][...] = row


def state_kernel(blocks, count, plan_ref, *refs):
    pieces, (master_ref, moment_ref, second_ref) = refs[:count], refs[count : count + 3]
    new_master, new_moment, new_second, folded = refs[count + 3 :]
    fold(blocks, plan_ref, pieces, folded)
    for p in range(folded.shape[0]):
        new_master[p], new_moment[p], new_second[p] = adam_update(
            folded[p], master_ref[p], moment_ref[p], second_ref[p]
        )


def unpack_kernel(blocks, place_ref, *refs):
    parts, out_ref = refs[:-1], refs[-1]
    place = place_ref[...].T
    if len(parts) > 1:
        parts = [parts[blocks.index(d)] for d in range(len(parts))]
    for cols in columns(out_ref.shape[1]):
        rows = [p[:, cols] for p in parts]
        rows = rows[0] if len(rows) == 1 else jnp.concatenate(rows, axis=0)
        out_ref[:, cols] = dot(place, rows, NN).astype(BF16)


def order_kernel(blocks, *refs):
    e = lax.axis_index("expert")
    for i, d in enumerate(blocks):
        refs[-1][e ^ d] = refs[i][...]


def swap(x, axis, mask):
    size = lax.axis_size(axis)
    return lax.ppermute(x, axis, [(i, i ^ mask) for i in range(size)])


def order(n):
    return [0, n // 2, *(d for d in range(1, n) if d != n // 2)]


def crossing(n):
    return [0, *range(n // 2, n - 1), *range(1, n // 2), n - 1]


def by_turns(n):
    return [0, *(d for r in range(n // 2) for d in (n // 2 + r, r + 1))][:n]


def exchange(blocks, ways):
    return [swap(blocks[d], "expert", d) if d else blocks[d] for d in ways]


def exchange_whole(x):
    flip = jnp.arange(x.shape[0], dtype=jnp.int32) ^ lax.axis_index("expert")
    x = jnp.take(x, flip, axis=0)
    x = lax.all_to_all(x, "expert", split_axis=0, concat_axis=0, tiled=True)
    return jnp.take(x, flip, axis=0)


def after(*values):
    return lax.optimization_barrier(values)


def body(
    tokens, out_grad, routing, plan, gate_weight, up_weight, down_weight, master, moment, second
):
    n, m = lax.axis_size("expert"), lax.axis_size("slot")
    owned, width = tokens.shape
    capacity = 2 * owned // n
    part = down_weight.shape[1]
    owner = part // n
    rows = n * capacity
    few = capacity % 16 == 0
    ways = order(n) if few else list(range(n))
    mixed = by_turns(n) if few else ways
    shape = jax.ShapeDtypeStruct

    weights = [jnp.swapaxes(w, 1, 2)[0] for w in (gate_weight, up_weight)] + [down_weight[0]]
    joined = jnp.concatenate(weights, axis=0)
    outs = [shape((rows, owned), BF16)]
    outs += [shape((2 * capacity, width), BF16)] * n if few else [shape((rows, width), BF16)] * 2
    place, *packed = call(
        functools.partial(pack_kernel, n, capacity, few),
        outs,
        (routing.reshape(1, owned), tokens, out_grad),
        name="pack_rows",
        flops=4 * owned * rows * width,
    )
    if few:
        blocks = exchange(packed, mixed)
    else:
        x, g = (
            exchange_whole(p.reshape(n, capacity, width)).reshape(rows, width) for p in packed
        )
        blocks = [jnp.concatenate((x, g), axis=0)]
    nb = len(blocks)

    held = {0: joined}
    for mask in [1 << i for i in range(1, m.bit_length() - 1)][::-1]:
        for r in sorted(held):
            held[r | mask] = swap(held[r], "slot", mask)
    near = [joined, swap(joined, "slot", 1)]
    blocks[1:], held = after(blocks[1:], [held[r] for r in range(2, m, 2)])
    high = [w for v in held for w in (v[: 2 * part], swap(v[: 2 * part], "slot", 1))]
    low = [w for v in held for w in (v[2 * part :], swap(v[2 * part :], "slot", 1))]
    nf = len(high)

    send, kept, partial = call(
        functools.partial(near_kernel, nb, 2),
        [shape((part, width), BF16), shape((part, width), BF16), shape((rows, width), F32)],
        (*blocks, *near),
        scratch=[pltpu.VMEM((2, part, rows), BF16), pltpu.VMEM((rows, 4 * part), BF16)],
        name="near_units",
        flops=24 * rows * width * part,
    )
    first = [kept, swap(send, "slot", 1)]
    high, partial = after(high, partial)
    send, keep, a, b = call(
        functools.partial(hidden_kernel, nb, nf),
        [shape((nf // 2 * part, width), BF16)] * 2 + [shape((nf, part, rows), F32)] * 2,
        (*blocks, *high),
        scratch=[pltpu.VMEM((nf, part, rows), BF16)],
        name="far_units",
        flops=6 * rows * width * part * nf,
    )
    got = swap(send, "slot", 1)
    dx = call(
        functools.partial(back_kernel, nb, nf),
        [shape((r.shape[0] // 2, width), BF16) for r in blocks],
        (*blocks, *high, *low, a, b, partial),
        scratch=[pltpu.VMEM((rows, nf * 2 * part), BF16)],
        name="input_gradient",
        flops=6 * rows * width * part * nf,
    )
    got, dx = after(got, list(dx))
    rest = call(
        add_kernel,
        [shape((part, width), BF16)] * (nf // 2),
        (keep, got),
        name="add_pair",
    )
    rest = [swap(r, "slot", 2 * i) for i, r in enumerate(rest, 1)]
    owner = part // n
    if few:
        back = crossing(n)
        dx = dict(zip(mixed, dx, strict=True))
        returned = exchange(dx, back[:-1])
        ahead = n // 2
        returned[1:ahead], rest = after(returned[1:ahead], rest)
    pieces = call(
        functools.partial(cut_kernel, len(first) + len(rest), ways),
        [shape((owner, width), BF16)] * n if few else [shape((part, width), BF16)],
        (*first, *rest),
        scratch=[pltpu.VMEM((part, width), F32)],
        name="cut_gradient",
    )
    if few:
        arrived = exchange(dict(zip(ways, pieces, strict=True)), ways)
        if PIECES:
            dx[n - 1], arrived[PIECES] = after(dx[n - 1], arrived[PIECES])
        returned += exchange(dx, back[-1:])
    else:
        back = ways
        returned = [exchange_whole(dx[0].reshape(n, capacity, width)).reshape(rows, width)]
        flip = jnp.arange(n, dtype=jnp.int32) ^ lax.axis_index("expert")
        arrived = [exchange_whole(jnp.take(pieces[0].reshape(n, owner, width), flip, axis=0))]
    state = (plan, *arrived, master, moment, second)
    outgoing = call(
        functools.partial(rows_kernel, ways, mixed, len(arrived)),
        [shape((owner, width), BF16)] * n if few else [shape((n, owner, width), BF16)],
        state,
        scratch=[pltpu.VMEM(master.shape, F32)],
        smem=(0,),
        name="new_rows",
        flops=NEWFLOPS,
    )
    if few and OUT:
        outgoing = list(outgoing)
        returned[-1], outgoing[OUT:] = after(returned[-1], outgoing[OUT:])
    new_master, new_moment, new_second = call(
        functools.partial(state_kernel, ways, len(arrived)),
        [shape(master.shape, F32)] * 3,
        state,
        scratch=[pltpu.VMEM(master.shape, F32)],
        smem=(0,),
        name="new_state",
    )
    (token_grad,) = call(
        functools.partial(unpack_kernel, back),
        [shape((owned, width), BF16)],
        (place, *returned),
        name="unpack_rows",
        flops=2 * owned * rows * width,
    )
    if few:
        (fresh,) = call(
            functools.partial(order_kernel, mixed),
            [shape((n, owner, width), BF16)],
            exchange(dict(zip(mixed, outgoing, strict=True)), mixed),
            name="order_rows",
        )
    else:
        fresh = exchange_whole(outgoing[0])
    return (token_grad, new_master, new_moment, new_second, fresh.reshape(1, part, width))


def solution(mesh):
    rows, state = P(("expert", "slot"), None), P(None, ("slot", "expert"), None)
    split, held = P("expert", None, "slot"), P("expert", "slot", None)
    return jax.shard_map(
        body,
        mesh=mesh,
        in_specs=(rows, rows, rows, P(), split, split, held, state, state, state),
        out_specs=(rows, state, state, state, held),
        check_vma=False,
    )
```

```python
import functools

import jax
import jax.numpy as jnp
from jax import lax
from jax.experimental import pallas as pl
from jax.experimental.pallas import tpu as pltpu
from jax.sharding import PartitionSpec as P

BF16 = jnp.bfloat16
F32 = jnp.float32
NT = (((1,), (1,)), ((), ()))
TN = (((0,), (0,)), ((), ()))
NN = (((1,), (0,)), ((), ()))
COLUMNS = 1024
PIECES = 6
OUT = 3
NEWFLOPS = 2 * 10**9


def dot(a, b, dims):
    return lax.dot_general(a, b, dims, preferred_element_type=F32)


def call(kernel, outs, args, scratch=(), smem=(), far=(), name=None, mib=40, flops=0):
    moved = sum(a.size * a.dtype.itemsize for a in args) + sum(
        o.size * o.dtype.itemsize for o in outs
    )
    return pl.pallas_call(
        kernel,
        out_shape=tuple(outs),
        in_specs=[
            pl.BlockSpec(
                memory_space=pltpu.SMEM if i in smem else pl.ANY if i in far else pltpu.VMEM
            )
            for i in range(len(args))
        ],
        out_specs=tuple(pl.BlockSpec(memory_space=pltpu.VMEM) for _ in outs),
        scratch_shapes=list(scratch),
        compiler_params=pltpu.CompilerParams(vmem_limit_bytes=mib * 2**20),
        cost_estimate=pl.CostEstimate(flops=flops, bytes_accessed=moved, transcendentals=0),
        name=name,
    )(*args)


def columns(width):
    step = min(COLUMNS, width)
    return [slice(c, c + step) for c in range(0, width, step)]


def pack_kernel(n, capacity, joint, r_ref, x_ref, g_ref, place_ref, *outs):
    e = lax.axis_index("expert")
    owned, width = x_ref.shape
    rel = r_ref[...] ^ e
    block = lax.broadcasted_iota(jnp.int32, (n, owned), 0)
    match = (rel == block).astype(F32)
    upper = lax.broadcasted_iota(jnp.int32, (owned, owned), 0) <= lax.broadcasted_iota(
        jnp.int32, (owned, owned), 1
    )
    count = dot(match.astype(BF16), upper.astype(BF16), NN)
    pos = jnp.sum(match * (count - 1.0 + (block * capacity).astype(F32)), axis=0, keepdims=True)
    spot = lax.broadcasted_iota(jnp.int32, (n * capacity, owned), 0)
    place = (pos.astype(jnp.int32) == spot).astype(BF16)
    place_ref[...] = place
    for half, ref in enumerate((x_ref, g_ref)):
        for cols in columns(width):
            packed = dot(place, ref[:, cols], NN).astype(BF16)
            if joint:
                for d in range(n):
                    outs[d][half * capacity : (half + 1) * capacity, cols] = packed[
                        d * capacity : (d + 1) * capacity
                    ]
            else:
                outs[half][:, cols] = packed


def halves(blocks, half):
    parts = []
    for ref in blocks:
        rows = ref.shape[0] // 2
        parts.append(ref[half * rows : (half + 1) * rows])
    return parts[0] if len(parts) == 1 else jnp.concatenate(parts, axis=0)


def parted(weights, count):
    if len(weights) == 2 * count:
        return weights[:count], weights[count:]
    part = weights[0].shape[0] // 3
    return [w.at[: 2 * part] for w in weights], [w.at[2 * part :] for w in weights]


def forward(high, x):
    both = dot(high[...], x, NT)
    part = both.shape[0] // 2
    gate, up = both[:part], both[part:]
    sig = jax.nn.sigmoid(gate)
    silu = gate * sig
    return (silu * up).astype(BF16), up * sig * (1.0 + gate * (1.0 - sig)), silu


def weight_gradient(hidden, g, send_ref, keep_ref):
    part = hidden.shape[1]
    for r in range(hidden.shape[0]):
        rows = slice(r // 2 * part, (r // 2 + 1) * part)
        for cols in columns(g.shape[1]):
            value = dot(hidden[r], g[:, cols], NN).astype(BF16)
            (send_ref if r % 2 else keep_ref)[rows, cols] = value


def turn(low, g, a, b):
    dh = dot(low[...], g, NT)
    both = jnp.concatenate(((dh * a).astype(BF16), (dh * b).astype(BF16)), axis=0)
    return both.T


def input_gradient(turned, highs, cols):
    wide = highs[0].shape[0]
    total = None
    for r, high in enumerate(highs):
        term = dot(turned[:, r * wide : (r + 1) * wide], high[:, cols], NN)
        total = term if total is None else total + term
    return total


def near_kernel(nb, nw, *refs):
    blocks, weights = refs[:nb], refs[nb : nb + nw]
    send_ref, keep_ref, partial_ref, hidden, turned = refs[nb + nw :]
    x, g = halves(blocks, 0), halves(blocks, 1)
    highs, lows = parted(weights, nw)
    wide = highs[0].shape[0]
    for r in range(nw):
        hidden[r], a, b = forward(highs[r], x)
        turned[:, r * wide : (r + 1) * wide] = turn(lows[r], g, a, b)
    weight_gradient(hidden, g, send_ref, keep_ref)
    for cols in columns(g.shape[1]):
        partial_ref[:, cols] = input_gradient(turned, highs, cols)


def hidden_kernel(nb, nw, *refs):
    blocks, highs = refs[:nb], refs[nb : nb + nw]
    send_ref, keep_ref, a_ref, b_ref, hidden = refs[nb + nw :]
    x, g = halves(blocks, 0), halves(blocks, 1)
    for r in range(nw):
        hidden[r], a_ref[r], b_ref[r] = forward(highs[r], x)
    weight_gradient(hidden, g, send_ref, keep_ref)


def back_kernel(nb, nw, *refs):
    blocks, (highs, lows) = refs[:nb], parted(refs[nb : nb + 2 * nw], nw)
    a_ref, b_ref, partial_ref = refs[nb + 2 * nw : nb + 2 * nw + 3]
    outs, turned = refs[nb + 2 * nw + 3 : -1], refs[-1]
    g = halves(blocks, 1)
    wide = highs[0].shape[0]
    for r in range(nw):
        turned[:, r * wide : (r + 1) * wide] = turn(lows[r], g, a_ref[r], b_ref[r])
    for cols in columns(g.shape[1]):
        total = (partial_ref[:, cols] + input_gradient(turned, highs, cols)).astype(BF16)
        start = 0
        for out in outs:
            out[:, cols] = total[start : start + out.shape[0]]
            start += out.shape[0]


def add_kernel(keep_ref, got_ref, *outs):
    part = outs[0].shape[0]
    for i, out in enumerate(outs):
        rows = slice(i * part, (i + 1) * part)
        out[...] = (keep_ref[rows].astype(F32) + got_ref[rows].astype(F32)).astype(BF16)


def cut_kernel(count, blocks, *refs):
    terms, outs, sums = refs[:count], refs[count:-1], refs[-1]
    e = lax.axis_index("expert")
    total = terms[0][...].astype(F32)
    for ref in terms[1:]:
        total = total + ref[...].astype(F32)
    if len(outs) == 1:
        outs[0][...] = total.astype(BF16)
        return
    sums[...] = total
    rows = outs[0].shape[0]
    for d, out in zip(blocks, outs, strict=True):
        out[...] = sums[pl.ds(pl.multiple_of((e ^ d) * rows, 8), rows)].astype(BF16)


def fold(blocks, plan_ref, pieces, folded):
    e = lax.axis_index("expert")
    folded[...] = jnp.zeros_like(folded)
    for i, d in enumerate(blocks):
        p = plan_ref[e ^ d]
        piece = pieces[0][i] if len(pieces) == 1 else pieces[i][...]
        folded[p] = folded[p] + piece.astype(F32)


def adam_update(folded, master, moment, second):
    new_moment = 0.9 * moment + 0.1 * folded
    new_second = 0.95 * second + 0.05 * folded * folded
    first_hat = new_moment * (1.0 / (1.0 - 0.9**10))
    second_hat = new_second * (1.0 / (1.0 - 0.95**10))
    new_master = master - 0.01 * (first_hat / (jnp.sqrt(second_hat) + 1e-08) + 0.1 * master)
    return new_master, new_moment, new_second


def rows_kernel(blocks, new, count, plan_ref, *refs):
    pieces, (master_ref, moment_ref, second_ref) = refs[:count], refs[count : count + 3]
    outs, folded = refs[count + 3 : -1], refs[-1]
    e = lax.axis_index("expert")
    fold(blocks, plan_ref, pieces, folded)
    for p in range(folded.shape[0]):
        folded[p] = adam_update(folded[p], master_ref[p], moment_ref[p], second_ref[p])[0]
    for i, d in enumerate(new):
        row = folded[plan_ref[e ^ d]].astype(BF16)
        if len(outs) == 1:
            outs[0][i] = row
        else:
            outs[i][...] = row


def state_kernel(blocks, count, plan_ref, *refs):
    pieces, (master_ref, moment_ref, second_ref) = refs[:count], refs[count : count + 3]
    new_master, new_moment, new_second, folded = refs[count + 3 :]
    fold(blocks, plan_ref, pieces, folded)
    for p in range(folded.shape[0]):
        new_master[p], new_moment[p], new_second[p] = adam_update(
            folded[p], master_ref[p], moment_ref[p], second_ref[p]
        )


def unpack_kernel(blocks, place_ref, *refs):
    parts, out_ref = refs[:-1], refs[-1]
    place = place_ref[...].T
    if len(parts) > 1:
        parts = [parts[blocks.index(d)] for d in range(len(parts))]
    for cols in columns(out_ref.shape[1]):
        rows = [p[:, cols] for p in parts]
        rows = rows[0] if len(rows) == 1 else jnp.concatenate(rows, axis=0)
        out_ref[:, cols] = dot(place, rows, NN).astype(BF16)


def order_kernel(blocks, *refs):
    e = lax.axis_index("expert")
    for i, d in enumerate(blocks):
        refs[-1][e ^ d] = refs[i][...]


def swap(x, axis, mask):
    size = lax.axis_size(axis)
    return lax.ppermute(x, axis, [(i, i ^ mask) for i in range(size)])


def order(n):
    return [0, n // 2, *(d for d in range(1, n) if d != n // 2)]


def crossing(n):
    return [0, *range(n // 2, n - 1), *range(1, n // 2), n - 1]


def by_turns(n):
    return [0, *(d for r in range(n // 2) for d in (n // 2 + r, r + 1))][:n]


def exchange(blocks, ways):
    return [swap(blocks[d], "expert", d) if d else blocks[d] for d in ways]


def exchange_whole(x):
    flip = jnp.arange(x.shape[0], dtype=jnp.int32) ^ lax.axis_index("expert")
    x = jnp.take(x, flip, axis=0)
    x = lax.all_to_all(x, "expert", split_axis=0, concat_axis=0, tiled=True)
    return jnp.take(x, flip, axis=0)


def after(*values):
    return lax.optimization_barrier(values)


def body(
    tokens, out_grad, routing, plan, gate_weight, up_weight, down_weight, master, moment, second
):
    n, m = lax.axis_size("expert"), lax.axis_size("slot")
    owned, width = tokens.shape
    capacity = 2 * owned // n
    part = down_weight.shape[1]
    owner = part // n
    rows = n * capacity
    few = capacity % 16 == 0
    ways = order(n) if few else list(range(n))
    mixed = by_turns(n) if few else ways
    shape = jax.ShapeDtypeStruct

    weights = [jnp.swapaxes(w, 1, 2)[0] for w in (gate_weight, up_weight)] + [down_weight[0]]
    joined = jnp.concatenate(weights, axis=0)
    outs = [shape((rows, owned), BF16)]
    outs += [shape((2 * capacity, width), BF16)] * n if few else [shape((rows, width), BF16)] * 2
    place, *packed = call(
        functools.partial(pack_kernel, n, capacity, few),
        outs,
        (routing.reshape(1, owned), tokens, out_grad),
        name="pack_rows",
        flops=4 * owned * rows * width,
    )
    if few:
        blocks = exchange(packed, mixed)
    else:
        x, g = (
            exchange_whole(p.reshape(n, capacity, width)).reshape(rows, width) for p in packed
        )
        blocks = [jnp.concatenate((x, g), axis=0)]
    nb = len(blocks)

    held = {0: joined}
    for mask in [1 << i for i in range(1, m.bit_length() - 1)][::-1]:
        for r in sorted(held):
            held[r | mask] = swap(held[r], "slot", mask)
    near = [joined, swap(joined, "slot", 1)]
    blocks[1:], held = after(blocks[1:], [held[r] for r in range(2, m, 2)])
    high = [w for v in held for w in (v[: 2 * part], swap(v[: 2 * part], "slot", 1))]
    low = [w for v in held for w in (v[2 * part :], swap(v[2 * part :], "slot", 1))]
    nf = len(high)

    send, kept, partial = call(
        functools.partial(near_kernel, nb, 2),
        [shape((part, width), BF16), shape((part, width), BF16), shape((rows, width), F32)],
        (*blocks, *near),
        scratch=[pltpu.VMEM((2, part, rows), BF16), pltpu.VMEM((rows, 4 * part), BF16)],
        name="near_units",
        flops=24 * rows * width * part,
    )
    first = [kept, swap(send, "slot", 1)]
    high, partial = after(high, partial)
    send, keep, a, b = call(
        functools.partial(hidden_kernel, nb, nf),
        [shape((nf // 2 * part, width), BF16)] * 2 + [shape((nf, part, rows), F32)] * 2,
        (*blocks, *high),
        scratch=[pltpu.VMEM((nf, part, rows), BF16)],
        name="far_units",
        flops=6 * rows * width * part * nf,
    )
    got = swap(send, "slot", 1)
    dx = call(
        functools.partial(back_kernel, nb, nf),
        [shape((r.shape[0] // 2, width), BF16) for r in blocks],
        (*blocks, *high, *low, a, b, partial),
        scratch=[pltpu.VMEM((rows, nf * 2 * part), BF16)],
        name="input_gradient",
        flops=6 * rows * width * part * nf,
    )
    got, dx = after(got, list(dx))
    rest = call(
        add_kernel,
        [shape((part, width), BF16)] * (nf // 2),
        (keep, got),
        name="add_pair",
    )
    rest = [swap(r, "slot", 2 * i) for i, r in enumerate(rest, 1)]
    owner = part // n
    if few:
        back = crossing(n)
        dx = dict(zip(mixed, dx, strict=True))
        returned = exchange(dx, back[:-1])
        ahead = n // 2
        returned[1:ahead], rest = after(returned[1:ahead], rest)
    pieces = call(
        functools.partial(cut_kernel, len(first) + len(rest), ways),
        [shape((owner, width), BF16)] * n if few else [shape((part, width), BF16)],
        (*first, *rest),
        scratch=[pltpu.VMEM((part, width), F32)],
        name="cut_gradient",
    )
    if few:
        arrived = exchange(dict(zip(ways, pieces, strict=True)), ways)
        if PIECES:
            dx[n - 1], arrived[PIECES] = after(dx[n - 1], arrived[PIECES])
        returned += exchange(dx, back[-1:])
    else:
        back = ways
        returned = [exchange_whole(dx[0].reshape(n, capacity, width)).reshape(rows, width)]
        flip = jnp.arange(n, dtype=jnp.int32) ^ lax.axis_index("expert")
        arrived = [exchange_whole(jnp.take(pieces[0].reshape(n, owner, width), flip, axis=0))]
    state = (plan, *arrived, master, moment, second)
    outgoing = call(
        functools.partial(rows_kernel, ways, mixed, len(arrived)),
        [shape((owner, width), BF16)] * n if few else [shape((n, owner, width), BF16)],
        state,
        scratch=[pltpu.VMEM(master.shape, F32)],
        smem=(0,),
        name="new_rows",
        flops=NEWFLOPS,
    )
    if few and OUT:
        outgoing = list(outgoing)
        returned[-1], outgoing[OUT:] = after(returned[-1], outgoing[OUT:])
    new_master, new_moment, new_second = call(
        functools.partial(state_kernel, ways, len(arrived)),
        [shape(master.shape, F32)] * 3,
        state,
        scratch=[pltpu.VMEM(master.shape, F32)],
        smem=(0,),
        name="new_state",
    )
    (token_grad,) = call(
        functools.partial(unpack_kernel, back),
        [shape((owned, width), BF16)],
        (place, *returned),
        name="unpack_rows",
        flops=2 * owned * rows * width,
    )
    if few:
        (fresh,) = call(
            functools.partial(order_kernel, mixed),
            [shape((n, owner, width), BF16)],
            exchange(dict(zip(mixed, outgoing, strict=True)), mixed),
            name="order_rows",
        )
    else:
        fresh = exchange_whole(outgoing[0])
    return (token_grad, new_master, new_moment, new_second, fresh.reshape(1, part, width))


def solution(mesh):
    rows, state = P(("expert", "slot"), None), P(None, ("slot", "expert"), None)
    split, held = P("expert", None, "slot"), P("expert", "slot", None)
    return jax.shard_map(
        body,
        mesh=mesh,
        in_specs=(rows, rows, rows, P(), split, split, held, state, state, state),
        out_specs=(rows, state, state, state, held),
        check_vma=False,
    )
```
